32 devices in a mesh: pool: 32 (over z, y, x, core).
Axes of the slice: x: 2, y: 2, z: 4, core: 2. Of those that a mesh axis runs over, the one named last changes fastest.
Arguments:
- queries: bfloat16 [32, 2, 3584], P('pool'), may hold values from -120 to 120
- kv_pool: bfloat16 [1024, 256, 2, 512], P('pool'), may hold values from -6 to 6
- lengths: int32 [32], P('pool'), may hold values from 1 to 8190, 131072 in all
- block_table: int32 [1024], P('pool'), may hold values from 0 to 1023, as said below
Outputs:
- attended: bfloat16 [32, 2, 3584], P('pool')
The draws below stay inside these ranges and needn't reach their ends.
Inputs may be any that keep to these rules, and one draw needn't show every extreme that they name: `block_table`: a permutation of the pool blocks; with the requests numbered in groups of 1 per owner index o and G groups, the entry at place j of the 32 entries of group o is a block numbered from ((o + s_j) mod G) * 32 to that + 31, where s_j = (j * G) // 32, except s_0 = 1 when G > 32. The pool holds positions 0 to lengths + 1 of each request.
All inputs are finite; a program needn't handle non-finite values. No bound on the sum of `lengths` on one device may be relied on, other than what follows from the above.
Results may differ from the reference program's by a relative error of at most 0.0095.
Values may be sent and summed in bfloat16 or wider, within the bound.
A program may use at most 192 MiB of HBM per device.

```python
import math
import jax
import jax.numpy as jnp
import numpy as np
from jax import lax

KVH = 4
GROUP = 7
HEAD = 128
BLOCK = 256
MAXBLK = 32
REQ_DEV = 1
REQUESTS = 32
POOL_DEV = 32
POOL = 1024


def draw_queries(key, part):
    key = jax.random.fold_in(key, 11)
    first_key = jax.random.fold_in(key, 0)
    drawn_rows = jnp.clip(jax.random.normal(first_key, (REQUESTS, 2, KVH, GROUP, HEAD), jnp.float32), -6.0, 6.0)
    return drawn_rows.reshape(REQUESTS, 2, KVH * GROUP * HEAD).astype(jnp.bfloat16)


def draw_kv_pool(key, part):
    key = jax.random.fold_in(key, 23)
    first_key = jax.random.fold_in(key, 0)
    third_key = jax.random.fold_in(key, 2)
    cache_keys = jnp.clip(jax.random.normal(first_key, (POOL, BLOCK, KVH, HEAD), jnp.float32), -6.0, 6.0)
    cache_values = jnp.clip(jax.random.normal(third_key, (POOL, BLOCK, KVH, HEAD), jnp.float32), -6.0, 6.0)
    stacked = jnp.stack([cache_keys, cache_values], axis=2)
    return stacked.reshape(POOL, BLOCK, 2, KVH * HEAD).astype(jnp.bfloat16)


def draw_block_table(key, part):
    key = jax.random.fold_in(key, 37)
    owners = REQUESTS // REQ_DEV
    first_step = 1 if owners > POOL_DEV else 0
    device_keys = jax.random.split(key, owners)
    orders = jax.vmap(lambda one_key: jax.random.permutation(one_key, jnp.arange(POOL_DEV, dtype=jnp.int32)))(device_keys)
    owner_ids = jnp.arange(owners, dtype=jnp.int32)[:, None]
    places = jnp.arange(POOL_DEV, dtype=jnp.int32)[None, :]
    steps_away = jnp.where(places == 0, first_step, places * owners // POOL_DEV).astype(jnp.int32)
    holders = (owner_ids + steps_away) % owners
    slots = orders[holders, jnp.broadcast_to(places, holders.shape)]
    return (holders * POOL_DEV + slots).reshape(REQUESTS * MAXBLK).astype(jnp.int32)


def split_up(count, total, reach, slope):
    portions = [(1 << 20) // math.isqrt(grade ** slope) + 1 for grade in range(2, count + 1)]
    spare, given = total - reach - (count - 1), [1] * (count - 1)
    while spare > 0:
        free = [i for i in range(count - 1) if given[i] < reach]
        whole, remaining = sum([portions[i] for i in free]), spare
        for i in free:
            more = min(reach - given[i], max(1, remaining * portions[i] // whole), spare)
            given[i] = given[i] + more
            spare = spare - more
    return np.array([reach] + given)


def ragged(key, amount, total, reach, lean):
    if amount == 2:
        one = jax.random.randint(key, (), max(1, total - reach), min(reach, total - 1) + 1)
        return jnp.stack([one, total - one])
    sizes = jnp.asarray(split_up(amount, total, reach, lean), jnp.int32)
    pairs = (amount - 1) // 2
    giver, receiver = sizes[1:1 + 2 * pairs:2], sizes[2:2 + 2 * pairs:2]
    slack = jnp.minimum(giver - 1, reach - receiver)
    moved = jax.random.randint(jax.random.fold_in(key, 1), (pairs,), 0, 1 << 20) % (slack + 1)
    sizes = sizes.at[1:1 + 2 * pairs:2].set(giver - moved).at[2:2 + 2 * pairs:2].set(receiver + moved)
    return sizes[jax.random.permutation(jax.random.fold_in(key, 2), amount)]


def setup_inputs(seed: int = 0) -> dict:
    streams_of = jax.random.split(jax.random.key(seed), 5)
    queries = draw_queries(jax.random.fold_in(streams_of[4], 71), 0)
    kv_pool = draw_kv_pool(jax.random.fold_in(streams_of[4], 71), 0)
    lengths = ragged(streams_of[2], REQUESTS, REQUESTS * (MAXBLK * BLOCK // 2), MAXBLK * BLOCK - 2, 2).astype(jnp.int32)
    block_table = draw_block_table(jax.random.fold_in(streams_of[4], 71), 0)
    return dict(queries=queries, kv_pool=kv_pool, lengths=lengths, block_table=block_table)


def reference(queries, kv_pool, lengths, block_table):
    table_rows = block_table.reshape(REQUESTS, MAXBLK)
    score_scale = 1.0 / (HEAD ** 0.5)

    def attend_one(request_data):
        request_query, length, blocks = request_data
        gathered = kv_pool[blocks]
        cache_keys = gathered[:, :, 0, :].reshape(MAXBLK * BLOCK, KVH, HEAD).astype(jnp.float32)
        cache_values = gathered[:, :, 1, :].reshape(MAXBLK * BLOCK, KVH, HEAD).astype(jnp.float32)
        query_rows = request_query.reshape(2, KVH, GROUP, HEAD).astype(jnp.float32)
        scores = jnp.einsum("tkgd,pkd->tkgp", query_rows, cache_keys, precision=lax.Precision.HIGHEST) * score_scale
        positions = jnp.arange(MAXBLK * BLOCK, dtype=jnp.int32)
        visible_end = length + 1 + jnp.arange(2, dtype=jnp.int32)
        visible = positions[None, :] < visible_end[:, None]
        scores = jnp.where(visible[:, None, None, :], scores, -jnp.inf)
        row_max = jnp.max(scores, axis=-1, keepdims=True)
        unscaled = jnp.exp(scores - row_max)
        total = jnp.sum(unscaled, axis=-1)
        weights = lax.optimization_barrier(unscaled.astype(jnp.bfloat16)).astype(jnp.float32)
        numerator = jnp.einsum("tkgp,pkd->tkgd", weights, cache_values, precision=lax.Precision.HIGHEST)
        return (numerator / total[..., None]).reshape(2, KVH * GROUP * HEAD).astype(jnp.bfloat16)

    return lax.map(attend_one, (queries, lengths, table_rows))
```

```python
import functools

import jax
import jax.numpy as jnp
from jax import lax
from jax.experimental import pallas as pl
from jax.experimental.pallas import tpu as pltpu
from jax.sharding import PartitionSpec as P

KVH = 4
GROUP = 7
HEAD = 128
BLOCK = 256
ROWS = 16 * KVH
PLANE = 4
CORES = 2
M_ROW, L_ROW, L_LOW_ROW = 14, 15, 30
MASKED = -1e30
FLOOR = -1e20
SCALE = 1.0 / HEAD**0.5
MESH = pl.DeviceIdType.MESH


def kernel(
    n, slots, width,
    query_ref, lengths_ref, table_ref, pool_ref, out_ref,
    kv, every_query, meta, meta_scalar, spread, columns,
    core_send, core_recv, own_part, plane_send, plane_recv, plane_own, line_send, line_recv, line_own,
    kv_sem, scalar_sem,
    meta_line_s, meta_line_r, meta_plane_s, meta_plane_r, meta_core_s, meta_core_r,
    query_line_s, query_line_r, query_plane_s, query_plane_r, query_core_s, query_core_r,
    core_s, core_r, plane_s, plane_r, line_s, line_r,
):
    me = lax.axis_index("pool")
    depth = n // (PLANE * CORES)
    stride = n // width
    zz = me // (PLANE * CORES)
    pp = (me // CORES) % PLANE
    cc = me % CORES
    other = 1 - cc

    def device(z, p, c):
        return ((z * PLANE + p) * CORES + c,)

    line_to = [(zz + i) % depth for i in range(depth)]
    line_from = [(zz + depth - i) % depth for i in range(depth)]
    plane_to = [(pp + i) % PLANE for i in range(PLANE)]
    plane_from = [(pp + PLANE - i) % PLANE for i in range(PLANE)]

    chunk = slots // 4
    kv_copies = []
    for part in range(4):
        for k in range(KVH):
            copy = pltpu.make_async_copy(
                pool_ref.at[pl.ds(part * chunk, chunk), :, :, pl.ds(k * HEAD, HEAD)],
                kv.at[k, pl.ds(part * chunk, chunk)],
                kv_sem.at[part, k],
            )
            copy.start()
            kv_copies.append(copy)

    barrier = pltpu.get_barrier_semaphore()
    peers = [device(line_to[i], pp, cc) for i in range(1, depth)]
    peers += [device(zz, plane_to[i], cc) for i in range(1, PLANE)]
    peers += [device(zz, pp, other)]
    for peer in peers:
        pl.semaphore_signal(barrier, inc=1, device_id=peer, device_id_type=MESH)

    lane = lax.broadcasted_iota(jnp.int32, (1, HEAD), 1)
    own_meta = jnp.where(lane == width, lengths_ref[0], 0)
    for j in range(width):
        own_meta = jnp.where(lane == j, table_ref[j], own_meta)
    meta[cc, pp, zz] = own_meta

    spread[...] = jnp.zeros_like(spread)
    own_query = query_ref[0].astype(jnp.float32)
    for h in range(KVH * GROUP):
        row = 16 * (h // GROUP) + 2 * (h % GROUP)
        spread[row : row + 2, :] = own_query[:, h * HEAD : (h + 1) * HEAD]
    every_query[zz, cc, pp] = spread[...].astype(jnp.bfloat16)

    col = lax.broadcasted_iota(jnp.int32, (16, 2 * BLOCK), 1)
    row = lax.broadcasted_iota(jnp.int32, (16, 2 * BLOCK), 0)
    columns[...] = jnp.where(col % 2 == 0, col - 2 * (row % 2), 1 << 24)

    pl.semaphore_wait(barrier, len(peers))

    def send(src, dst, s, r, to):
        copy = pltpu.make_async_remote_copy(
            src_ref=src, dst_ref=dst, send_sem=s, recv_sem=r, device_id=to, device_id_type=MESH
        )
        return copy

    sent = []

    def go(copy):
        copy.start()
        sent.append(copy)

    def arrive(dst, s, r):
        send(dst, dst, s, r, device(zz, pp, other)).wait_recv()

    for i in range(1, depth):
        ref = meta.at[cc, pp, zz]
        go(send(ref, ref, meta_line_s.at[i - 1], meta_line_r.at[i - 1], device(line_to[i], pp, cc)))
    for i in range(1, depth):
        ref = every_query.at[zz, cc, pp]
        go(send(ref, ref, query_line_s.at[i - 1], query_line_r.at[i - 1], device(line_to[i], pp, cc)))

    def query_to_plane(i):
        ref = every_query.at[line_from[i], cc, pp]
        for d in range(1, PLANE):
            go(send(ref, ref, query_plane_s.at[i, d - 1], query_plane_r.at[i, d - 1],
                    device(zz, plane_to[d], cc)))

    query_to_plane(0)
    for i in range(1, depth):
        arrive(meta.at[cc, pp, line_from[i]], meta_line_s.at[i - 1], meta_line_r.at[i - 1])
    for d in range(1, PLANE):
        ref = meta.at[cc, pp]
        go(send(ref, ref, meta_plane_s.at[d - 1], meta_plane_r.at[d - 1], device(zz, plane_to[d], cc)))
    for i in range(1, depth):
        arrive(every_query.at[line_from[i], cc, pp], query_line_s.at[i - 1], query_line_r.at[i - 1])
        query_to_plane(i)
    for d in range(1, PLANE):
        arrive(meta.at[cc, plane_from[d]], meta_plane_s.at[d - 1], meta_plane_r.at[d - 1])
    ref = meta.at[cc]
    go(send(ref, ref, meta_core_s.at[0], meta_core_r.at[0], device(zz, pp, other)))
    order = list(range(1, depth)) + [0]
    for i in [0] + list(range(1, depth)):
        for d in range(1, PLANE):
            arrive(every_query.at[line_from[i], cc, plane_from[d]],
                   query_plane_s.at[i, d - 1], query_plane_r.at[i, d - 1])
        ref = every_query.at[line_from[i], cc]
        go(send(ref, ref, query_core_s.at[i], query_core_r.at[i], device(zz, pp, other)))
    arrive(meta.at[other], meta_core_s.at[0], meta_core_r.at[0])
    to_scalar = pltpu.make_async_copy(meta, meta_scalar, scalar_sem)
    to_scalar.start()
    to_scalar.wait()
    for copy in kv_copies:
        copy.wait()

    rows = kv.reshape(KVH, slots, 2 * BLOCK, HEAD)
    row_id = lax.broadcasted_iota(jnp.int32, (ROWS, HEAD), 0)
    lane_id = lax.broadcasted_iota(jnp.int32, (ROWS, HEAD), 1)
    eye = row_id == lane_id

    def as_column(vector):
        return jnp.sum(jnp.where(eye, vector, 0.0), axis=1, keepdims=True)

    def encode(numer, peak, total):
        high = total.astype(jnp.bfloat16).astype(jnp.float32)
        numer = jnp.where(row_id == M_ROW, peak, numer)
        numer = jnp.where(row_id == L_ROW, high, numer)
        return jnp.where(row_id == L_LOW_ROW, total - high, numer)

    def merge(states):
        states = [s.astype(jnp.float32) for s in states]
        peaks = [s[M_ROW : M_ROW + 1] for s in states]
        totals = [s[L_ROW : L_ROW + 1] + s[L_LOW_ROW : L_LOW_ROW + 1] for s in states]
        peak = functools.reduce(jnp.maximum, peaks)
        shrink = [jnp.exp(p - peak) for p in peaks]
        total = sum(a * b for a, b in zip(shrink, totals))
        numer = sum(as_column(a) * s for a, s in zip(shrink, states))
        return numer, peak, total

    def attend(z, c, p):
        request = (z * PLANE + p) * CORES + c
        away = (me + n - request) % n
        place = away if stride == 1 else jnp.where(away == 1, 0, away // stride)
        slot = lax.rem(meta_scalar[c, p, z, 0, place], slots)
        limit = 2 * (meta_scalar[c, p, z, 0, width] + 1 - place * BLOCK)
        visible = columns[...] < limit
        numers = []
        peak_row = jnp.zeros((1, HEAD), jnp.float32)
        total_row = jnp.zeros((1, HEAD), jnp.float32)
        for k in range(KVH):
            query = every_query[z, c, p, 16 * k : 16 * (k + 1), :]
            block = rows[k, slot]
            scores = lax.dot_general(
                query, block, (((1,), (1,)), ((), ())), preferred_element_type=jnp.float32
            )
            scores = jnp.where(visible, scores * SCALE, MASKED)
            peak = jnp.maximum(jnp.max(scores, axis=1, keepdims=True), FLOOR)
            peak = peak.astype(jnp.bfloat16).astype(jnp.float32)
            unscaled = jnp.exp(scores - peak)
            total = jnp.sum(unscaled, axis=1, keepdims=True)
            shifted = jnp.concatenate(
                [pltpu.roll(unscaled[:, a : a + HEAD], 1, 1) for a in range(0, 2 * BLOCK, HEAD)], axis=1
            )
            numers.append(
                jnp.dot(shifted.astype(jnp.bfloat16), block, preferred_element_type=jnp.float32)
            )
            diagonal = eye[16 * k : 16 * (k + 1)]
            peak_row += jnp.sum(jnp.where(diagonal, peak, 0.0), axis=0, keepdims=True)
            total_row += jnp.sum(jnp.where(diagonal, total, 0.0), axis=0, keepdims=True)
        return encode(jnp.concatenate(numers, axis=0), peak_row, total_row)

    def attend_into(store, z, c, p):
        if stride == 1:
            store(attend(z, c, p))
            return
        away = (me + n - ((z * PLANE + p) * CORES + c)) % n
        held = (away == 1) | ((away % stride == 0) & (away > 0))

        @pl.when(held)
        def _():
            store(attend(z, c, p))

        @pl.when(jnp.logical_not(held))
        def _():
            store(jnp.where(row_id == M_ROW, FLOOR, jnp.zeros((ROWS, HEAD), jnp.float32)))

    def compute(i):
        z = line_from[i]
        arrive(every_query.at[z, other], query_core_s.at[i], query_core_r.at[i])

        @pl.loop(0, PLANE)
        def _(p):
            def store(state):
                core_send[i, p] = state.astype(jnp.bfloat16)

            attend_into(store, z, other, p)

        go(send(core_send.at[i], core_recv.at[i], core_s.at[i], core_r.at[i], device(zz, pp, other)))

        @pl.loop(0, PLANE)
        def _(p):
            def store(state):
                own_part[i, p] = state

            attend_into(store, z, cc, p)

    def reduce_core(i):
        arrive(core_recv.at[i], core_s.at[i], core_r.at[i])
        for d in list(range(1, PLANE)) + [0]:
            p = plane_to[d]
            state = encode(*merge([own_part[i, p], core_recv[i, p]]))
            if d == 0:
                plane_own[i] = state
            else:
                plane_send[i, d - 1] = state.astype(jnp.bfloat16)
                go(send(plane_send.at[i, d - 1], plane_recv.at[i, d - 1],
                        plane_s.at[i, d - 1], plane_r.at[i, d - 1], device(zz, plane_to[d], cc)))

    def reduce_plane(i):
        for d in range(1, PLANE):
            arrive(plane_recv.at[i, d - 1], plane_s.at[i, d - 1], plane_r.at[i, d - 1])
        state = encode(*merge([plane_own[i]] + [plane_recv[i, d] for d in range(PLANE - 1)]))
        if i == 0:
            line_own[...] = state
        else:
            line_send[i - 1] = state.astype(jnp.bfloat16)
            go(send(line_send.at[i - 1], line_recv.at[i - 1], line_s.at[i - 1], line_r.at[i - 1],
                    device(line_from[i], pp, cc)))

    for step in range(depth + 2):
        if step < depth:
            compute(order[step])
        if 1 <= step <= depth:
            reduce_core(order[step - 1])
        if step >= 2:
            reduce_plane(order[step - 2])

    for i in range(1, depth):
        arrive(line_recv.at[i - 1], line_s.at[i - 1], line_r.at[i - 1])
    numer, _, total = merge([line_own[...]] + [line_recv[i] for i in range(depth - 1)])
    spread[...] = numer / as_column(total)
    for h in range(KVH * GROUP):
        row = 16 * (h // GROUP) + 2 * (h % GROUP)
        out_ref[0, :, h * HEAD : (h + 1) * HEAD] = spread[row : row + 2, :].astype(jnp.bfloat16)
    for copy in sent:
        copy.wait_send()


def body(n, queries, kv_pool, lengths, block_table):
    slots, width = kv_pool.shape[0], block_table.shape[0]
    depth = n // (PLANE * CORES)
    state, bf16, f32 = (ROWS, HEAD), jnp.bfloat16, jnp.float32
    dma = pltpu.SemaphoreType.DMA
    smem = pl.BlockSpec(memory_space=pltpu.SMEM)
    vmem = pl.BlockSpec(memory_space=pltpu.VMEM)
    return pl.pallas_call(
        functools.partial(kernel, n, slots, width),
        out_shape=jax.ShapeDtypeStruct(queries.shape, queries.dtype),
        in_specs=[vmem, smem, smem, pl.BlockSpec(memory_space=pl.ANY)],
        out_specs=vmem,
        scratch_shapes=[
            pltpu.VMEM((KVH, slots, BLOCK, 2, HEAD), bf16),
            pltpu.VMEM((depth, CORES, PLANE) + state, bf16),
            pltpu.VMEM((CORES, PLANE, depth, 1, HEAD), jnp.int32),
            pltpu.SMEM((CORES, PLANE, depth, 1, HEAD), jnp.int32),
            pltpu.VMEM(state, f32),
            pltpu.VMEM((16, 2 * BLOCK), jnp.int32),
            pltpu.VMEM((depth, PLANE) + state, bf16),
            pltpu.VMEM((depth, PLANE) + state, bf16),
            pltpu.VMEM((depth, PLANE) + state, f32),
            pltpu.VMEM((depth, PLANE - 1) + state, bf16),
            pltpu.VMEM((depth, PLANE - 1) + state, bf16),
            pltpu.VMEM((depth,) + state, f32),
            pltpu.VMEM((depth - 1,) + state, bf16),
            pltpu.VMEM((depth - 1,) + state, bf16),
            pltpu.VMEM(state, f32),
            dma((4, KVH)),
            dma,
            dma((depth - 1,)), dma((depth - 1,)), dma((PLANE - 1,)), dma((PLANE - 1,)), dma((1,)), dma((1,)),
            dma((depth - 1,)), dma((depth - 1,)), dma((depth, PLANE - 1)), dma((depth, PLANE - 1)),
            dma((depth,)), dma((depth,)),
            dma((depth,)), dma((depth,)), dma((depth, PLANE - 1)), dma((depth, PLANE - 1)),
            dma((depth - 1,)), dma((depth - 1,)),
        ],
        compiler_params=pltpu.CompilerParams(
            collective_id=0, has_side_effects=True, vmem_limit_bytes=48 * 1024 * 1024
        ),
    )(queries, lengths, block_table, kv_pool)


def solution(mesh):
    placed = (P("pool", None, None), P("pool", None, None, None), P("pool"), P("pool"))
    return jax.shard_map(
        functools.partial(body, mesh.shape["pool"]),
        mesh=mesh, in_specs=placed, out_specs=P("pool", None, None), check_vma=False,
    )
```

```python
import functools

import jax
import jax.numpy as jnp
from jax import lax
from jax.experimental import pallas as pl
from jax.experimental.pallas import tpu as pltpu
from jax.sharding import PartitionSpec as P

KVH = 4
GROUP = 7
HEAD = 128
BLOCK = 256
ROWS = 16 * KVH
PLANE = 4
CORES = 2
M_ROW, L_ROW, L_LOW_ROW = 14, 15, 30
MASKED = -1e30
FLOOR = -1e20
UNROLL = 4
SCALE = 1.0 / HEAD**0.5
MESH = pl.DeviceIdType.MESH


def places(n):
    me = lax.axis_index("pool")
    return me, me // (PLANE * CORES), (me // CORES) % PLANE, me % CORES


def remote(src, dst, s, r, to):
    return pltpu.make_async_remote_copy(
        src_ref=src, dst_ref=dst, send_sem=s, recv_sem=r, device_id=to, device_id_type=MESH
    )


def greet(peers):
    barrier = pltpu.get_barrier_semaphore()
    for peer in peers:
        pl.semaphore_signal(barrier, inc=1, device_id=peer, device_id_type=MESH)
    return lambda: pl.semaphore_wait(barrier, len(peers))


class Grid:
    def __init__(self, n):
        self.me, self.z, self.p, self.c = places(n)
        self.depth = n // (PLANE * CORES)
        self.other = 1 - self.c
        self.line_to = [(self.z + i) % self.depth for i in range(self.depth)]
        self.line_from = [(self.z + self.depth - i) % self.depth for i in range(self.depth)]
        self.plane_to = [(self.p + i) % PLANE for i in range(PLANE)]
        self.plane_from = [(self.p + PLANE - i) % PLANE for i in range(PLANE)]
        self.sent = []

    def at(self, z, p, c):
        return ((z * PLANE + p) * CORES + c,)

    def line(self, z):
        return self.at(z, self.p, self.c)

    def plane(self, p):
        return self.at(self.z, p, self.c)

    def core(self):
        return self.at(self.z, self.p, self.other)

    def peers(self):
        peers = [self.line(z) for z in self.line_to[1:]]
        return peers + [self.plane(p) for p in self.plane_to[1:]] + [self.core()]

    def go(self, src, dst, s, r, to):
        copy = remote(src, dst, s, r, to)
        copy.start()
        self.sent.append(copy)

    def arrive(self, dst, s, r):
        remote(dst, dst, s, r, self.core()).wait_recv()

    def finish(self):
        for copy in self.sent:
            copy.wait_send()


def gather_kernel(
    n, width,
    query_ref, lengths_ref, table_ref, every_query, meta,
    spread, length_scalar, table_scalar, small_sem,
    meta_line_s, meta_line_r, meta_plane_s, meta_plane_r, meta_core_s, meta_core_r,
    query_line_s, query_line_r, query_plane_s, query_plane_r, query_core_s, query_core_r,
):
    g = Grid(n)
    zz, pp, cc, depth = g.z, g.p, g.c, g.depth
    greeted = greet(g.peers())
    small = [
        pltpu.make_async_copy(lengths_ref, length_scalar, small_sem.at[0]),
        pltpu.make_async_copy(table_ref, table_scalar, small_sem.at[1]),
    ]
    for copy in small:
        copy.start()

    spread[...] = jnp.zeros_like(spread)
    own_query = query_ref[0].astype(jnp.float32)
    for h in range(KVH * GROUP):
        row = 16 * (h // GROUP) + 2 * (h % GROUP)
        spread[row : row + 2, :] = own_query[:, h * HEAD : (h + 1) * HEAD]
    every_query[zz, cc, pp] = spread[...].astype(jnp.bfloat16)
    for copy in small:
        copy.wait()
    lane = lax.broadcasted_iota(jnp.int32, (1, HEAD), 1)
    own_meta = jnp.where(lane == width, length_scalar[0], 0)
    for j in range(width):
        own_meta = jnp.where(lane == j, table_scalar[j], own_meta)
    meta[cc, pp, zz] = own_meta
    greeted()

    def query_to_plane(i):
        ref = every_query.at[g.line_from[i], cc, pp]
        for d in range(1, PLANE):
            g.go(ref, ref, query_plane_s.at[i, d - 1], query_plane_r.at[i, d - 1], g.plane(g.plane_to[d]))

    for i in range(1, depth):
        ref = every_query.at[zz, cc, pp]
        g.go(ref, ref, query_line_s.at[i - 1], query_line_r.at[i - 1], g.line(g.line_to[i]))
    for i in range(1, depth):
        ref = meta.at[cc, pp, zz]
        g.go(ref, ref, meta_line_s.at[i - 1], meta_line_r.at[i - 1], g.line(g.line_to[i]))
    query_to_plane(0)
    for i in range(1, depth):
        g.arrive(every_query.at[g.line_from[i], cc, pp], query_line_s.at[i - 1], query_line_r.at[i - 1])
        query_to_plane(i)
    for i in range(1, depth):
        g.arrive(meta.at[cc, pp, g.line_from[i]], meta_line_s.at[i - 1], meta_line_r.at[i - 1])
    for d in range(1, PLANE):
        ref = meta.at[cc, pp]
        g.go(ref, ref, meta_plane_s.at[d - 1], meta_plane_r.at[d - 1], g.plane(g.plane_to[d]))
    for i in range(depth):
        for d in range(1, PLANE):
            g.arrive(every_query.at[g.line_from[i], cc, g.plane_from[d]],
                     query_plane_s.at[i, d - 1], query_plane_r.at[i, d - 1])
        ref = every_query.at[g.line_from[i], cc]
        g.go(ref, ref, query_core_s.at[i], query_core_r.at[i], g.core())
    for d in range(1, PLANE):
        g.arrive(meta.at[cc, g.plane_from[d]], meta_plane_s.at[d - 1], meta_plane_r.at[d - 1])
    ref = meta.at[cc]
    g.go(ref, ref, meta_core_s.at[0], meta_core_r.at[0], g.core())
    for i in range(depth):
        g.arrive(every_query.at[g.line_from[i], g.other], query_core_s.at[i], query_core_r.at[i])
    g.arrive(meta.at[g.other], meta_core_s.at[0], meta_core_r.at[0])
    g.finish()


def state_ids():
    row_id = lax.broadcasted_iota(jnp.int32, (ROWS, HEAD), 0)
    return row_id, row_id == lax.broadcasted_iota(jnp.int32, (ROWS, HEAD), 1)


def encode(numer, peak, total):
    row_id, _ = state_ids()
    high = total.astype(jnp.bfloat16).astype(jnp.float32)
    numer = jnp.where(row_id == M_ROW, peak, numer)
    numer = jnp.where(row_id == L_ROW, high, numer)
    return jnp.where(row_id == L_LOW_ROW, total - high, numer)


def attend_kernel(
    n, slots, width,
    query_ref, meta_ref, pool_ref, out_ref,
    kv, columns, meta_scalar, held_place, count_ref, kv_sem, scalar_sem,
):
    me = lax.axis_index("pool")
    stride = n // width
    to_scalar = pltpu.make_async_copy(meta_ref, meta_scalar, scalar_sem)
    to_scalar.start()
    col = lax.broadcasted_iota(jnp.int32, (16, 2 * BLOCK), 1)
    row = lax.broadcasted_iota(jnp.int32, (16, 2 * BLOCK), 0)
    columns[...] = jnp.where(col % 2 == 0, col - 2 * (row % 2), 1 << 24)
    row_id, eye = state_ids()
    empty = jnp.where(row_id == M_ROW, FLOOR, jnp.zeros((ROWS, HEAD), jnp.float32)).astype(out_ref.dtype)
    depth = n // (PLANE * CORES)
    for z in range(depth):
        for c in range(CORES):
            for p in range(PLANE):
                out_ref[z, c, p] = empty

    def locate(place):
        step = place if stride == 1 else jnp.where(place == 0, 1, place * stride)
        request = lax.rem(me + n - step, n)
        return request // (PLANE * CORES), lax.rem(request // CORES, PLANE), lax.rem(request, CORES)

    to_scalar.wait()

    def pool_copies(index, slot):
        return [
            pltpu.make_async_copy(
                pool_ref.at[slot, :, :, pl.ds(k * HEAD, HEAD)], kv.at[k, index], kv_sem.at[k, index]
            )
            for k in range(KVH)
        ]

    count_ref[0] = 0

    @pl.loop(0, width)
    def _(place):
        z, p, c = locate(place)
        length = meta_scalar[c, p, z, 0, width]

        @pl.when(place * BLOCK < length + 2)
        def _():
            index = count_ref[0]
            held_place[index] = place
            for copy in pool_copies(index, lax.rem(meta_scalar[c, p, z, 0, place], slots)):
                copy.start()
            count_ref[0] = index + 1

    count = count_ref[0]
    rows = kv.reshape(KVH, slots, 2 * BLOCK, HEAD)

    def attend(index):
        place = held_place[index]
        z, p, c = locate(place)
        limit = 2 * (meta_scalar[c, p, z, 0, width] + 1 - place * BLOCK)
        visible = columns[...] < limit
        visible = jnp.concatenate([visible, visible], axis=0)
        numers = []
        peak_row = jnp.zeros((1, HEAD), jnp.float32)
        total_row = jnp.zeros((1, HEAD), jnp.float32)
        blank = jnp.zeros((16, HEAD), jnp.bfloat16)
        for k in range(0, KVH, 2):
            first = query_ref[z, c, p, 16 * k : 16 * (k + 1), :]
            second = query_ref[z, c, p, 16 * (k + 1) : 16 * (k + 2), :]
            query = jnp.concatenate(
                [jnp.concatenate([first, blank], axis=1), jnp.concatenate([blank, second], axis=1)], axis=0
            )
            block = jnp.concatenate([rows[k, index], rows[k + 1, index]], axis=1)
            scores = lax.dot_general(
                query, block, (((1,), (1,)), ((), ())), preferred_element_type=jnp.float32
            )
            scores = jnp.where(visible, scores * SCALE, MASKED)
            peak = jnp.maximum(jnp.max(scores, axis=1, keepdims=True), FLOOR)
            peak = peak.astype(jnp.bfloat16).astype(jnp.float32)
            unscaled = jnp.exp(scores - peak)
            total = jnp.sum(unscaled, axis=1, keepdims=True)
            shifted = jnp.concatenate(
                [pltpu.roll(unscaled[:, a : a + HEAD], 1, 1) for a in range(0, 2 * BLOCK, HEAD)], axis=1
            )
            both = jnp.dot(shifted.astype(jnp.bfloat16), block, preferred_element_type=jnp.float32)
            numers += [both[:16, :HEAD], both[16:, HEAD:]]
            diagonal = eye[16 * k : 16 * (k + 2)]
            peak_row += jnp.sum(jnp.where(diagonal, peak, 0.0), axis=0, keepdims=True)
            total_row += jnp.sum(jnp.where(diagonal, total, 0.0), axis=0, keepdims=True)
        state = encode(jnp.concatenate(numers, axis=0), peak_row, total_row)
        return (z, c, p), state.astype(out_ref.dtype)

    @pl.loop(0, (count + UNROLL - 1) // UNROLL)
    def _(step):
        for u in range(UNROLL):
            index = step * UNROLL + u

            @pl.when(index < count)
            def _():
                for copy in pool_copies(index, 0):
                    copy.wait()

        done = [attend(jnp.minimum(step * UNROLL + u, count - 1)) for u in range(UNROLL)]
        for (z, c, p), state in done:
            out_ref[z, c, p] = state


def reduce_kernel(
    n, part_ref, out_ref,
    spread, core_recv, plane_send, plane_recv, plane_own, line_send, line_recv, line_own,
    core_s, core_r, plane_s, plane_r, line_s, line_r,
):
    g = Grid(n)
    depth = g.depth
    greet(g.peers())()
    _, eye = state_ids()

    def as_column(vector):
        return jnp.sum(jnp.where(eye, vector, 0.0), axis=1, keepdims=True)

    def merge(states):
        states = [s.astype(jnp.float32) for s in states]
        peaks = [s[M_ROW : M_ROW + 1] for s in states]
        totals = [s[L_ROW : L_ROW + 1] + s[L_LOW_ROW : L_LOW_ROW + 1] for s in states]
        peak = functools.reduce(jnp.maximum, peaks)
        shrink = [jnp.exp(p - peak) for p in peaks]
        total = sum(a * b for a, b in zip(shrink, totals))
        numer = sum(as_column(a) * s for a, s in zip(shrink, states))
        return numer, peak, total

    order = list(range(1, depth)) + [0]
    for i in order:
        g.go(part_ref.at[g.line_from[i], g.other], core_recv.at[i], core_s.at[i], core_r.at[i], g.core())

    def reduce_core(i):
        g.arrive(core_recv.at[i], core_s.at[i], core_r.at[i])
        for d in list(range(1, PLANE)) + [0]:
            p = g.plane_to[d]
            state = encode(*merge([part_ref[g.line_from[i], g.c, p], core_recv[i, p]]))
            if d == 0:
                plane_own[i] = state
            else:
                plane_send[i, d - 1] = state.astype(jnp.bfloat16)
                g.go(plane_send.at[i, d - 1], plane_recv.at[i, d - 1],
                     plane_s.at[i, d - 1], plane_r.at[i, d - 1], g.plane(p))

    def reduce_plane(i):
        for d in range(1, PLANE):
            g.arrive(plane_recv.at[i, d - 1], plane_s.at[i, d - 1], plane_r.at[i, d - 1])
        state = encode(*merge([plane_own[i]] + [plane_recv[i, d] for d in range(PLANE - 1)]))
        if i == 0:
            line_own[...] = state
        else:
            line_send[i - 1] = state.astype(jnp.bfloat16)
            g.go(line_send.at[i - 1], line_recv.at[i - 1], line_s.at[i - 1], line_r.at[i - 1],
                 g.line(g.line_from[i]))

    for i in order:
        reduce_core(i)
    for i in order:
        reduce_plane(i)
    for i in range(1, depth):
        g.arrive(line_recv.at[i - 1], line_s.at[i - 1], line_r.at[i - 1])
    numer, _, total = merge([line_own[...]] + [line_recv[i] for i in range(depth - 1)])
    spread[...] = numer / as_column(total)
    for h in range(KVH * GROUP):
        row = 16 * (h // GROUP) + 2 * (h % GROUP)
        out_ref[0, :, h * HEAD : (h + 1) * HEAD] = spread[row : row + 2, :].astype(jnp.bfloat16)
    g.finish()


def body(n, queries, kv_pool, lengths, block_table):
    slots, width = kv_pool.shape[0], block_table.shape[0]
    depth = n // (PLANE * CORES)
    state, bf16, f32, i32 = (ROWS, HEAD), jnp.bfloat16, jnp.float32, jnp.int32
    dma = pltpu.SemaphoreType.DMA
    vmem, anywhere = pl.BlockSpec(memory_space=pltpu.VMEM), pl.BlockSpec(memory_space=pl.ANY)
    every = jax.ShapeDtypeStruct((depth, CORES, PLANE) + state, bf16)
    meta_shape = (CORES, PLANE, depth, 1, HEAD)

    def params(**more):
        return pltpu.CompilerParams(has_side_effects=True, vmem_limit_bytes=48 * 1024 * 1024, **more)

    every_query, meta = pl.pallas_call(
        functools.partial(gather_kernel, n, width),
        out_shape=[every, jax.ShapeDtypeStruct(meta_shape, i32)],
        in_specs=[vmem, anywhere, anywhere],
        out_specs=[vmem, vmem],
        scratch_shapes=[
            pltpu.VMEM(state, f32), pltpu.SMEM((1,), i32), pltpu.SMEM((width,), i32), dma((2,)),
            dma((depth - 1,)), dma((depth - 1,)), dma((PLANE - 1,)), dma((PLANE - 1,)), dma((1,)), dma((1,)),
            dma((depth - 1,)), dma((depth - 1,)), dma((depth, PLANE - 1)), dma((depth, PLANE - 1)),
            dma((depth,)), dma((depth,)),
        ],
        compiler_params=params(collective_id=0),
    )(queries, lengths, block_table)
    parts = pl.pallas_call(
        functools.partial(attend_kernel, n, slots, width),
        out_shape=every,
        in_specs=[vmem, anywhere, anywhere],
        out_specs=vmem,
        scratch_shapes=[
            pltpu.VMEM((KVH, slots, BLOCK, 2, HEAD), bf16),
            pltpu.VMEM((16, 2 * BLOCK), i32),
            pltpu.SMEM(meta_shape, i32),
            pltpu.SMEM((width,), i32), pltpu.SMEM((1,), i32),
            dma((KVH, slots)), dma,
        ],
        compiler_params=params(),
    )(every_query, meta, kv_pool)
    return pl.pallas_call(
        functools.partial(reduce_kernel, n),
        out_shape=jax.ShapeDtypeStruct(queries.shape, queries.dtype),
        in_specs=[vmem],
        out_specs=vmem,
        scratch_shapes=[
            pltpu.VMEM(state, f32),
            pltpu.VMEM((depth, PLANE) + state, bf16),
            pltpu.VMEM((depth, PLANE - 1) + state, bf16),
            pltpu.VMEM((depth, PLANE - 1) + state, bf16),
            pltpu.VMEM((depth,) + state, f32),
            pltpu.VMEM((depth - 1,) + state, bf16),
            pltpu.VMEM((depth - 1,) + state, bf16),
            pltpu.VMEM(state, f32),
            dma((depth,)), dma((depth,)), dma((depth, PLANE - 1)), dma((depth, PLANE - 1)),
            dma((depth - 1,)), dma((depth - 1,)),
        ],
        compiler_params=params(collective_id=1),
    )(parts)


def solution(mesh):
    placed = (P("pool", None, None), P("pool", None, None, None), P("pool"), P("pool"))
    return jax.shard_map(
        functools.partial(body, mesh.shape["pool"]),
        mesh=mesh, in_specs=placed, out_specs=P("pool", None, None), check_vma=False,
    )
```

```python
import functools

import jax
import jax.numpy as jnp
from jax import lax
from jax.experimental import pallas as pl
from jax.experimental.pallas import tpu as pltpu
from jax.sharding import PartitionSpec as P

KVH = 4
GROUP = 7
HEAD = 128
BLOCK = 256
ROWS = 16 * KVH
PLANE = 4
CORES = 2
M_ROW, L_ROW, L_LOW_ROW = 14, 15, 30
MASKED = -1e30
FLOOR = -1e20
UNROLL = 4
SCALE = 1.0 / HEAD**0.5
MESH = pl.DeviceIdType.MESH


def places():
    me = lax.axis_index("pool")
    chip = lax.div(me, CORES)
    z = lax.div(chip, PLANE)
    return me, z, chip - z * PLANE, me - chip * CORES


def wrap(value, size):
    return jnp.where(value >= size, value - size, value)


def remote(src, dst, s, r, to):
    return pltpu.make_async_remote_copy(
        src_ref=src, dst_ref=dst, send_sem=s, recv_sem=r, device_id=to, device_id_type=MESH
    )


def greet(peers):
    barrier = pltpu.get_barrier_semaphore()
    for peer in peers:
        pl.semaphore_signal(barrier, inc=1, device_id=peer, device_id_type=MESH)
    return lambda: pl.semaphore_wait(barrier, len(peers))


class Grid:
    def __init__(self, n):
        self.me, self.z, self.p, self.c = places()
        self.depth = n // (PLANE * CORES)
        self.other = 1 - self.c
        self.line_to = [wrap(self.z + i, self.depth) for i in range(self.depth)]
        self.line_from = [wrap(self.z + self.depth - i, self.depth) for i in range(self.depth)]
        self.plane_to = [wrap(self.p + i, PLANE) for i in range(PLANE)]
        self.plane_from = [wrap(self.p + PLANE - i, PLANE) for i in range(PLANE)]
        self.sent = []

    def at(self, z, p, c):
        return ((z * PLANE + p) * CORES + c,)

    def line(self, z):
        return self.at(z, self.p, self.c)

    def plane(self, p):
        return self.at(self.z, p, self.c)

    def core(self):
        return self.at(self.z, self.p, self.other)

    def peers(self):
        peers = [self.line(z) for z in self.line_to[1:]]
        return peers + [self.plane(p) for p in self.plane_to[1:]] + [self.core()]

    def go(self, src, dst, s, r, to):
        copy = remote(src, dst, s, r, to)
        copy.start()
        self.sent.append(copy)

    def arrive(self, dst, s, r):
        remote(dst, dst, s, r, self.core()).wait_recv()

    def finish(self):
        for copy in self.sent:
            copy.wait_send()


def gather_kernel(
    n, width,
    query_ref, lengths_ref, table_ref, every_query, meta,
    spread, held_query, length_scalar, table_scalar, small_sem,
    meta_line_s, meta_line_r, meta_plane_s, meta_plane_r, meta_core_s, meta_core_r,
    query_line_s, query_line_r, query_plane_s, query_plane_r, query_core_s, query_core_r,
):
    g = Grid(n)
    zz, pp, cc, depth = g.z, g.p, g.c, g.depth
    greeted = greet(g.peers())
    small = [
        pltpu.make_async_copy(lengths_ref, length_scalar, small_sem.at[0]),
        pltpu.make_async_copy(table_ref, table_scalar, small_sem.at[1]),
        pltpu.make_async_copy(query_ref, held_query, small_sem.at[2]),
    ]
    for copy in small:
        copy.start()

    spread[...] = jnp.zeros_like(spread)
    for copy in small:
        copy.wait()
    own_query = held_query[0].astype(jnp.float32)
    for h in range(KVH * GROUP):
        row = 16 * (h // GROUP) + 2 * (h % GROUP)
        spread[row : row + 2, :] = own_query[:, h * HEAD : (h + 1) * HEAD]
    every_query[zz, cc, pp] = spread[...].astype(jnp.bfloat16)
    lane = lax.broadcasted_iota(jnp.int32, (1, HEAD), 1)
    own_meta = jnp.where(lane == width, length_scalar[0], 0)
    for j in range(width):
        own_meta = jnp.where(lane == j, table_scalar[j], own_meta)
    meta[cc, pp, zz] = own_meta
    greeted()

    def query_to_plane(i):
        ref = every_query.at[g.line_from[i], cc, pp]
        for d in range(1, PLANE):
            g.go(ref, ref, query_plane_s.at[i, d - 1], query_plane_r.at[i, d - 1], g.plane(g.plane_to[d]))

    for i in range(1, depth):
        ref = every_query.at[zz, cc, pp]
        g.go(ref, ref, query_line_s.at[i - 1], query_line_r.at[i - 1], g.line(g.line_to[i]))
    for i in range(1, depth):
        ref = meta.at[cc, pp, zz]
        g.go(ref, ref, meta_line_s.at[i - 1], meta_line_r.at[i - 1], g.line(g.line_to[i]))
    query_to_plane(0)
    for i in range(1, depth):
        g.arrive(every_query.at[g.line_from[i], cc, pp], query_line_s.at[i - 1], query_line_r.at[i - 1])
        query_to_plane(i)
    for i in range(1, depth):
        g.arrive(meta.at[cc, pp, g.line_from[i]], meta_line_s.at[i - 1], meta_line_r.at[i - 1])
    for d in range(1, PLANE):
        ref = meta.at[cc, pp]
        g.go(ref, ref, meta_plane_s.at[d - 1], meta_plane_r.at[d - 1], g.plane(g.plane_to[d]))
    for i in range(depth):
        for d in range(1, PLANE):
            g.arrive(every_query.at[g.line_from[i], cc, g.plane_from[d]],
                     query_plane_s.at[i, d - 1], query_plane_r.at[i, d - 1])
        ref = every_query.at[g.line_from[i], cc]
        g.go(ref, ref, query_core_s.at[i], query_core_r.at[i], g.core())
    for d in range(1, PLANE):
        g.arrive(meta.at[cc, g.plane_from[d]], meta_plane_s.at[d - 1], meta_plane_r.at[d - 1])
    ref = meta.at[cc]
    g.go(ref, ref, meta_core_s.at[0], meta_core_r.at[0], g.core())
    for i in range(depth):
        g.arrive(every_query.at[g.line_from[i], g.other], query_core_s.at[i], query_core_r.at[i])
    g.arrive(meta.at[g.other], meta_core_s.at[0], meta_core_r.at[0])
    g.finish()


def state_ids():
    row_id = lax.broadcasted_iota(jnp.int32, (ROWS, HEAD), 0)
    return row_id, row_id == lax.broadcasted_iota(jnp.int32, (ROWS, HEAD), 1)


def encode(numer, peak, total):
    row_id, _ = state_ids()
    high = total.astype(jnp.bfloat16).astype(jnp.float32)
    numer = jnp.where(row_id == M_ROW, peak, numer)
    numer = jnp.where(row_id == L_ROW, high, numer)
    return jnp.where(row_id == L_LOW_ROW, total - high, numer)


def attend_kernel(
    n, slots, width,
    query_ref, meta_ref, pool_ref, out_ref,
    kv, columns, meta_scalar, held_at, held_limit, count_ref, kv_sem, scalar_sem,
):
    me = lax.axis_index("pool")
    stride = n // width
    to_scalar = pltpu.make_async_copy(meta_ref, meta_scalar, scalar_sem)
    to_scalar.start()
    col = lax.broadcasted_iota(jnp.int32, (16, 2 * BLOCK), 1)
    row = lax.broadcasted_iota(jnp.int32, (16, 2 * BLOCK), 0)
    columns[...] = jnp.where(col % 2 == 0, col - 2 * (row % 2), 1 << 24)
    row_id, eye = state_ids()
    empty = jnp.where(row_id == M_ROW, FLOOR, jnp.zeros((ROWS, HEAD), jnp.float32)).astype(out_ref.dtype)
    for request in range(n):
        out_ref[request] = empty
    depth = n // (PLANE * CORES)
    assert (PLANE, CORES) == (4, 2) and slots & (slots - 1) == 0

    def locate(place):
        step = place if stride == 1 else jnp.where(place == 0, 1, place * stride)
        request = me - step
        request = jnp.where(request < 0, request + n, request)
        return request >> 3, (request >> 1) & 3, request & 1

    to_scalar.wait()

    def pool_copies(index, slot):
        return [
            pltpu.make_async_copy(
                pool_ref.at[slot, :, :, pl.ds(k * HEAD, HEAD)], kv.at[k, index], kv_sem.at[k, index]
            )
            for k in range(KVH)
        ]

    count_ref[0] = 0

    @pl.loop(0, width)
    def _(place):
        z, p, c = locate(place)
        line = (c * PLANE + p) * depth + z
        length = meta_scalar[line, 0, width]

        @pl.when(place * BLOCK < length + 2)
        def _():
            index = count_ref[0]
            held_at[index] = (z * CORES + c) * PLANE + p
            held_limit[index] = 2 * (length + 1 - place * BLOCK)
            for copy in pool_copies(index, meta_scalar[line, 0, place] & (slots - 1)):
                copy.start()
            count_ref[0] = index + 1

    count = count_ref[0]
    rows = kv.reshape(KVH, slots, 2 * BLOCK, HEAD)

    def attend(index):
        at = held_at[index]
        visible = columns[...] < held_limit[index]
        visible = jnp.concatenate([visible, visible], axis=0)
        numers = []
        peak_row = jnp.zeros((1, HEAD), jnp.float32)
        total_row = jnp.zeros((1, HEAD), jnp.float32)
        blank = jnp.zeros((16, HEAD), jnp.bfloat16)
        for k in range(0, KVH, 2):
            first = query_ref[at, 16 * k : 16 * (k + 1), :]
            second = query_ref[at, 16 * (k + 1) : 16 * (k + 2), :]
            query = jnp.concatenate(
                [jnp.concatenate([first, blank], axis=1), jnp.concatenate([blank, second], axis=1)], axis=0
            )
            block = jnp.concatenate([rows[k, index], rows[k + 1, index]], axis=1)
            scores = lax.dot_general(
                query, block, (((1,), (1,)), ((), ())), preferred_element_type=jnp.float32
            )
            scores = jnp.where(visible, scores * SCALE, MASKED)
            peak = jnp.maximum(jnp.max(scores, axis=1, keepdims=True), FLOOR)
            peak = peak.astype(jnp.bfloat16).astype(jnp.float32)
            unscaled = jnp.exp(scores - peak)
            total = jnp.sum(unscaled, axis=1, keepdims=True)
            shifted = jnp.concatenate(
                [pltpu.roll(unscaled[:, a : a + HEAD], 1, 1) for a in range(0, 2 * BLOCK, HEAD)], axis=1
            )
            both = jnp.dot(shifted.astype(jnp.bfloat16), block, preferred_element_type=jnp.float32)
            numers += [both[:16, :HEAD], both[16:, HEAD:]]
            diagonal = eye[16 * k : 16 * (k + 2)]
            peak_row += jnp.sum(jnp.where(diagonal, peak, 0.0), axis=0, keepdims=True)
            total_row += jnp.sum(jnp.where(diagonal, total, 0.0), axis=0, keepdims=True)
        state = encode(jnp.concatenate(numers, axis=0), peak_row, total_row)
        return at, state.astype(out_ref.dtype)

    @pl.loop(0, (count + UNROLL - 1) // UNROLL)
    def _(step):
        for u in range(UNROLL):
            index = step * UNROLL + u

            @pl.when(index < count)
            def _():
                for copy in pool_copies(index, 0):
                    copy.wait()

        done = [attend(jnp.minimum(step * UNROLL + u, count - 1)) for u in range(UNROLL)]
        for at, state in done:
            out_ref[at] = state


def reduce_kernel(
    n, part_ref, out_ref,
    spread, core_recv, plane_send, plane_recv, plane_own, line_send, line_recv, line_own,
    core_s, core_r, plane_s, plane_r, line_s, line_r,
):
    g = Grid(n)
    depth = g.depth
    greet(g.peers())()
    _, eye = state_ids()

    def as_column(vector):
        return jnp.sum(jnp.where(eye, vector, 0.0), axis=1, keepdims=True)

    def merge(states):
        states = [s.astype(jnp.float32) for s in states]
        peaks = [s[M_ROW : M_ROW + 1] for s in states]
        totals = [s[L_ROW : L_ROW + 1] + s[L_LOW_ROW : L_LOW_ROW + 1] for s in states]
        peak = functools.reduce(jnp.maximum, peaks)
        shrink = [jnp.exp(p - peak) for p in peaks]
        total = sum(a * b for a, b in zip(shrink, totals))
        numer = sum(as_column(a) * s for a, s in zip(shrink, states))
        return numer, peak, total

    order = list(range(1, depth)) + [0]
    for i in order:
        g.go(part_ref.at[g.line_from[i], g.other], core_recv.at[i], core_s.at[i], core_r.at[i], g.core())

    def reduce_core(i):
        g.arrive(core_recv.at[i], core_s.at[i], core_r.at[i])
        for d in list(range(1, PLANE)) + [0]:
            p = g.plane_to[d]
            state = encode(*merge([part_ref[g.line_from[i], g.c, p], core_recv[i, p]]))
            if d == 0:
                plane_own[i] = state
            else:
                plane_send[i, d - 1] = state.astype(jnp.bfloat16)
                g.go(plane_send.at[i, d - 1], plane_recv.at[i, d - 1],
                     plane_s.at[i, d - 1], plane_r.at[i, d - 1], g.plane(p))

    def reduce_plane(i):
        for d in range(1, PLANE):
            g.arrive(plane_recv.at[i, d - 1], plane_s.at[i, d - 1], plane_r.at[i, d - 1])
        state = encode(*merge([plane_own[i]] + [plane_recv[i, d] for d in range(PLANE - 1)]))
        if i == 0:
            line_own[...] = state
        else:
            line_send[i - 1] = state.astype(jnp.bfloat16)
            g.go(line_send.at[i - 1], line_recv.at[i - 1], line_s.at[i - 1], line_r.at[i - 1],
                 g.line(g.line_from[i]))

    for i in order:
        reduce_core(i)
    for i in order:
        reduce_plane(i)
    for i in range(1, depth):
        g.arrive(line_recv.at[i - 1], line_s.at[i - 1], line_r.at[i - 1])
    numer, _, total = merge([line_own[...]] + [line_recv[i] for i in range(depth - 1)])
    spread[...] = numer / as_column(total)
    for h in range(KVH * GROUP):
        row = 16 * (h // GROUP) + 2 * (h % GROUP)
        out_ref[0, :, h * HEAD : (h + 1) * HEAD] = spread[row : row + 2, :].astype(jnp.bfloat16)
    g.finish()


def body(n, queries, kv_pool, lengths, block_table):
    slots, width = kv_pool.shape[0], block_table.shape[0]
    depth = n // (PLANE * CORES)
    state, bf16, f32, i32 = (ROWS, HEAD), jnp.bfloat16, jnp.float32, jnp.int32
    dma = pltpu.SemaphoreType.DMA
    vmem, anywhere = pl.BlockSpec(memory_space=pltpu.VMEM), pl.BlockSpec(memory_space=pl.ANY)
    far = pl.BlockSpec(memory_space=pltpu.HBM)
    every = jax.ShapeDtypeStruct((depth, CORES, PLANE) + state, bf16)
    meta_shape = (CORES, PLANE, depth, 1, HEAD)

    def params(**more):
        return pltpu.CompilerParams(has_side_effects=True, vmem_limit_bytes=48 * 1024 * 1024, **more)

    every_query, meta = pl.pallas_call(
        functools.partial(gather_kernel, n, width),
        out_shape=[every, jax.ShapeDtypeStruct(meta_shape, i32)],
        in_specs=[far, far, far],
        out_specs=[vmem, vmem],
        scratch_shapes=[
            pltpu.VMEM(state, f32), pltpu.VMEM(queries.shape, bf16),
            pltpu.SMEM((1,), i32), pltpu.SMEM((width,), i32), dma((3,)),
            dma((depth - 1,)), dma((depth - 1,)), dma((PLANE - 1,)), dma((PLANE - 1,)), dma((1,)), dma((1,)),
            dma((depth - 1,)), dma((depth - 1,)), dma((depth, PLANE - 1)), dma((depth, PLANE - 1)),
            dma((depth,)), dma((depth,)),
        ],
        compiler_params=params(collective_id=0),
    )(queries, lengths, block_table)
    parts = pl.pallas_call(
        functools.partial(attend_kernel, n, slots, width),
        out_shape=jax.ShapeDtypeStruct((n,) + state, bf16),
        in_specs=[vmem, anywhere, anywhere],
        out_specs=vmem,
        scratch_shapes=[
            pltpu.VMEM((KVH, slots, BLOCK, 2, HEAD), bf16),
            pltpu.VMEM((16, 2 * BLOCK), i32),
            pltpu.SMEM((n, 1, HEAD), i32),
            pltpu.SMEM((width,), i32), pltpu.SMEM((width,), i32), pltpu.SMEM((1,), i32),
            dma((KVH, slots)), dma,
        ],
        compiler_params=params(),
    )(every_query.reshape((n,) + state), meta.reshape(n, 1, HEAD), kv_pool)
    return pl.pallas_call(
        functools.partial(reduce_kernel, n),
        out_shape=jax.ShapeDtypeStruct(queries.shape, queries.dtype),
        in_specs=[vmem],
        out_specs=vmem,
        scratch_shapes=[
            pltpu.VMEM(state, f32),
            pltpu.VMEM((depth, PLANE) + state, bf16),
            pltpu.VMEM((depth, PLANE - 1) + state, bf16),
            pltpu.VMEM((depth, PLANE - 1) + state, bf16),
            pltpu.VMEM((depth,) + state, f32),
            pltpu.VMEM((depth - 1,) + state, bf16),
            pltpu.VMEM((depth - 1,) + state, bf16),
            pltpu.VMEM(state, f32),
            dma((depth,)), dma((depth,)), dma((depth, PLANE - 1)), dma((depth, PLANE - 1)),
            dma((depth - 1,)), dma((depth - 1,)),
        ],
        compiler_params=params(collective_id=1),
    )(parts.reshape(every.shape))


def solution(mesh):
    placed = (P("pool", None, None), P("pool", None, None, None), P("pool"), P("pool"))
    return jax.shard_map(
        functools.partial(body, mesh.shape["pool"]),
        mesh=mesh, in_specs=placed, out_specs=P("pool", None, None), check_vma=False,
    )
```

```python
import functools

import jax
import jax.numpy as jnp
from jax import lax
from jax.experimental import pallas as pl
from jax.experimental.pallas import tpu as pltpu
from jax.sharding import PartitionSpec as P

KVH = 4
GROUP = 7
HEAD = 128
BLOCK = 256
ROWS = 16 * KVH
PLANE = 4
CORES = 2
M_ROW, L_ROW, L_LOW_ROW = 14, 15, 30
MASKED = -1e30
FLOOR = -1e20
UNROLL = 4
SCALE = 1.0 / HEAD**0.5
MESH = pl.DeviceIdType.MESH


def places():
    me = lax.axis_index("pool")
    chip = lax.div(me, CORES)
    z = lax.div(chip, PLANE)
    return me, z, chip - z * PLANE, me - chip * CORES


def wrap(value, size):
    return jnp.where(value >= size, value - size, value)


def remote(src, dst, s, r, to):
    return pltpu.make_async_remote_copy(
        src_ref=src, dst_ref=dst, send_sem=s, recv_sem=r, device_id=to, device_id_type=MESH
    )


def greet(peers):
    barrier = pltpu.get_barrier_semaphore()
    for peer in peers:
        pl.semaphore_signal(barrier, inc=1, device_id=peer, device_id_type=MESH)
    return lambda: pl.semaphore_wait(barrier, len(peers))


class Grid:
    def __init__(self, n):
        self.me, self.z, self.p, self.c = places()
        self.depth = n // (PLANE * CORES)
        self.other = 1 - self.c
        self.line_to = [wrap(self.z + i, self.depth) for i in range(self.depth)]
        self.line_from = [wrap(self.z + self.depth - i, self.depth) for i in range(self.depth)]
        self.plane_to = [wrap(self.p + i, PLANE) for i in range(PLANE)]
        self.plane_from = [wrap(self.p + PLANE - i, PLANE) for i in range(PLANE)]
        self.sent = []

    def at(self, z, p, c):
        return ((z * PLANE + p) * CORES + c,)

    def line(self, z):
        return self.at(z, self.p, self.c)

    def plane(self, p):
        return self.at(self.z, p, self.c)

    def core(self):
        return self.at(self.z, self.p, self.other)

    def peers(self):
        peers = [self.line(z) for z in self.line_to[1:]]
        return peers + [self.plane(p) for p in self.plane_to[1:]] + [self.core()]

    def go(self, src, dst, s, r, to):
        copy = remote(src, dst, s, r, to)
        copy.start()
        self.sent.append(copy)

    def arrive(self, dst, s, r):
        remote(dst, dst, s, r, self.core()).wait_recv()

    def finish(self):
        for copy in self.sent:
            copy.wait_send()


def gather_kernel(
    n, width,
    query_ref, lengths_ref, table_ref, every_query, meta,
    spread, held_query, length_scalar, table_scalar, small_sem,
    meta_line_s, meta_line_r, meta_plane_s, meta_plane_r, meta_core_s, meta_core_r,
    query_line_s, query_line_r, query_plane_s, query_plane_r, query_core_s, query_core_r,
):
    g = Grid(n)
    zz, pp, cc, depth = g.z, g.p, g.c, g.depth
    greeted = greet(g.peers())
    small = [
        pltpu.make_async_copy(lengths_ref, length_scalar, small_sem.at[0]),
        pltpu.make_async_copy(table_ref, table_scalar, small_sem.at[1]),
        pltpu.make_async_copy(query_ref, held_query, small_sem.at[2]),
    ]
    for copy in small:
        copy.start()

    spread[...] = jnp.zeros_like(spread)
    for copy in small:
        copy.wait()
    own_query = held_query[0].astype(jnp.float32)
    for h in range(KVH * GROUP):
        row = 16 * (h // GROUP) + 2 * (h % GROUP)
        spread[row : row + 2, :] = own_query[:, h * HEAD : (h + 1) * HEAD]
    every_query[zz, cc, pp] = spread[...].astype(jnp.bfloat16)
    lane = lax.broadcasted_iota(jnp.int32, (1, HEAD), 1)
    own_meta = jnp.where(lane == width, length_scalar[0], 0)
    for j in range(width):
        own_meta = jnp.where(lane == j, table_scalar[j], own_meta)
    meta[cc, pp, zz] = own_meta
    greeted()

    def query_to_plane(i):
        ref = every_query.at[g.line_from[i], cc, pp]
        for d in range(1, PLANE):
            g.go(ref, ref, query_plane_s.at[i, d - 1], query_plane_r.at[i, d - 1], g.plane(g.plane_to[d]))

    for i in range(1, depth):
        ref = every_query.at[zz, cc, pp]
        g.go(ref, ref, query_line_s.at[i - 1], query_line_r.at[i - 1], g.line(g.line_to[i]))
    for i in range(1, depth):
        ref = meta.at[cc, pp, zz]
        g.go(ref, ref, meta_line_s.at[i - 1], meta_line_r.at[i - 1], g.line(g.line_to[i]))
    query_to_plane(0)
    for i in range(1, depth):
        g.arrive(every_query.at[g.line_from[i], cc, pp], query_line_s.at[i - 1], query_line_r.at[i - 1])
        query_to_plane(i)
    for i in range(1, depth):
        g.arrive(meta.at[cc, pp, g.line_from[i]], meta_line_s.at[i - 1], meta_line_r.at[i - 1])
    for d in range(1, PLANE):
        ref = meta.at[cc, pp]
        g.go(ref, ref, meta_plane_s.at[d - 1], meta_plane_r.at[d - 1], g.plane(g.plane_to[d]))
    for i in range(depth):
        for d in range(1, PLANE):
            g.arrive(every_query.at[g.line_from[i], cc, g.plane_from[d]],
                     query_plane_s.at[i, d - 1], query_plane_r.at[i, d - 1])
        ref = every_query.at[g.line_from[i], cc]
        g.go(ref, ref, query_core_s.at[i], query_core_r.at[i], g.core())
    for d in range(1, PLANE):
        g.arrive(meta.at[cc, g.plane_from[d]], meta_plane_s.at[d - 1], meta_plane_r.at[d - 1])
    ref = meta.at[cc]
    g.go(ref, ref, meta_core_s.at[0], meta_core_r.at[0], g.core())
    for i in range(depth):
        g.arrive(every_query.at[g.line_from[i], g.other], query_core_s.at[i], query_core_r.at[i])
    g.arrive(meta.at[g.other], meta_core_s.at[0], meta_core_r.at[0])
    g.finish()


def state_ids():
    row_id = lax.broadcasted_iota(jnp.int32, (ROWS, HEAD), 0)
    return row_id, row_id == lax.broadcasted_iota(jnp.int32, (ROWS, HEAD), 1)


def encode(numer, peak, total):
    row_id, _ = state_ids()
    high = total.astype(jnp.bfloat16).astype(jnp.float32)
    numer = jnp.where(row_id == M_ROW, peak, numer)
    numer = jnp.where(row_id == L_ROW, high, numer)
    return jnp.where(row_id == L_LOW_ROW, total - high, numer)


def attend_kernel(
    n, slots, width,
    query_ref, meta_ref, pool_ref, out_ref,
    kv, columns, meta_scalar, held_at, held_limit, count_ref, kv_sem, scalar_sem,
):
    me = lax.axis_index("pool")
    stride = n // width
    to_scalar = pltpu.make_async_copy(meta_ref, meta_scalar, scalar_sem)
    to_scalar.start()
    row = lax.broadcasted_iota(jnp.int32, (2 * BLOCK, HEAD), 0)
    lane = lax.broadcasted_iota(jnp.int32, (2 * BLOCK, HEAD), 1)
    columns[...] = jnp.where(row % 2 == 0, row - 2 * (lane % 2), 1 << 24)
    row_id, _ = state_ids()
    empty = jnp.where(row_id == M_ROW, FLOOR, jnp.zeros((ROWS, HEAD), jnp.float32)).astype(out_ref.dtype)
    for request in range(n):
        out_ref[request] = empty
    depth = n // (PLANE * CORES)
    assert (PLANE, CORES) == (4, 2) and slots & (slots - 1) == 0

    def locate(place):
        step = place if stride == 1 else jnp.where(place == 0, 1, place * stride)
        request = me - step
        request = jnp.where(request < 0, request + n, request)
        return request >> 3, (request >> 1) & 3, request & 1

    to_scalar.wait()

    def pool_copies(index, slot):
        return [
            pltpu.make_async_copy(
                pool_ref.at[slot, :, :, pl.ds(k * HEAD, HEAD)], kv.at[k, index], kv_sem.at[k, index]
            )
            for k in range(KVH)
        ]

    count_ref[0] = 0

    @pl.loop(0, width)
    def _(place):
        z, p, c = locate(place)
        line = (c * PLANE + p) * depth + z
        length = meta_scalar[line, 0, width]

        @pl.when(place * BLOCK < length + 2)
        def _():
            index = count_ref[0]
            held_at[index] = (z * CORES + c) * PLANE + p
            held_limit[index] = 2 * (length + 1 - place * BLOCK)
            for copy in pool_copies(index, meta_scalar[line, 0, place] & (slots - 1)):
                copy.start()
            count_ref[0] = index + 1

    count = count_ref[0]
    rows = kv.reshape(KVH, slots, 2 * BLOCK, HEAD)

    lane_row = lax.broadcasted_iota(jnp.int32, (1, HEAD), 1)
    lane_group = lax.broadcasted_iota(jnp.int32, (HEAD, HEAD), 1) // 16

    def attend(indices):
        ats = [held_at[index] for index in indices]
        limit = jnp.where(lane_row < ROWS, held_limit[indices[0]], held_limit[indices[1]])
        pair = jnp.concatenate([query_ref[at] for at in ats], axis=0).astype(jnp.float32)
        pair = jnp.transpose(pair)
        scores = jnp.zeros((2 * BLOCK, HEAD), jnp.float32)
        for r in range(2):
            for k in range(0, KVH, 2):
                block = jnp.concatenate([rows[k, indices[r]], rows[k + 1, indices[r]]], axis=1)
                query = jnp.concatenate(
                    [jnp.where(lane_group == r * KVH + h, pair, 0.0) for h in (k, k + 1)], axis=0
                )
                scores += jnp.dot(block, query.astype(jnp.bfloat16), preferred_element_type=jnp.float32)
        scores = jnp.where(columns[...] < limit, scores * SCALE, MASKED)
        peak = jnp.maximum(jnp.max(scores, axis=0, keepdims=True), FLOOR)
        peak = peak.astype(jnp.bfloat16).astype(jnp.float32)
        unscaled = jnp.exp(scores - peak)
        total = jnp.sum(unscaled, axis=0, keepdims=True)
        shifted = pltpu.roll(unscaled.reshape(2 * BLOCK // 8, 8, HEAD), 1, 1).reshape(2 * BLOCK, HEAD)
        weights = jnp.transpose(shifted.astype(jnp.bfloat16))
        states = []
        for r in range(2):
            numers = []
            for k in range(0, KVH, 2):
                block = jnp.concatenate([rows[k, indices[r]], rows[k + 1, indices[r]]], axis=1)
                base = r * ROWS + 16 * k
                both = jnp.dot(weights[base : base + 32], block, preferred_element_type=jnp.float32)
                numers += [both[:16, :HEAD], both[16:, HEAD:]]
            if r == 1:
                peak, total = pltpu.roll(peak, ROWS, 1), pltpu.roll(total, ROWS, 1)
            state = encode(jnp.concatenate(numers, axis=0), peak, total)
            states.append((ats[r], state.astype(out_ref.dtype)))
        return states

    @pl.loop(0, (count + UNROLL - 1) // UNROLL)
    def _(step):
        for u in range(UNROLL):
            index = step * UNROLL + u

            @pl.when(index < count)
            def _():
                for copy in pool_copies(index, 0):
                    copy.wait()

        indices = [jnp.minimum(step * UNROLL + u, count - 1) for u in range(UNROLL)]
        done = [attend(indices[u : u + 2]) for u in range(0, UNROLL, 2)]
        for at, state in sum(done, []):
            out_ref[at] = state


def reduce_kernel(
    n, part_ref, out_ref,
    spread, core_recv, plane_send, plane_recv, plane_own, line_send, line_recv, line_own,
    core_s, core_r, plane_s, plane_r, line_s, line_r,
):
    g = Grid(n)
    depth = g.depth
    greet(g.peers())()
    _, eye = state_ids()

    def as_column(vector):
        return jnp.sum(jnp.where(eye, vector, 0.0), axis=1, keepdims=True)

    def merge(states):
        states = [s.astype(jnp.float32) for s in states]
        peaks = [s[M_ROW : M_ROW + 1] for s in states]
        totals = [s[L_ROW : L_ROW + 1] + s[L_LOW_ROW : L_LOW_ROW + 1] for s in states]
        peak = functools.reduce(jnp.maximum, peaks)
        shrink = [jnp.exp(p - peak) for p in peaks]
        total = sum(a * b for a, b in zip(shrink, totals))
        numer = sum(as_column(a) * s for a, s in zip(shrink, states))
        return numer, peak, total

    order = list(range(1, depth)) + [0]
    for i in order:
        g.go(part_ref.at[g.line_from[i], g.other], core_recv.at[i], core_s.at[i], core_r.at[i], g.core())

    def reduce_core(i):
        g.arrive(core_recv.at[i], core_s.at[i], core_r.at[i])
        for d in list(range(1, PLANE)) + [0]:
            p = g.plane_to[d]
            state = encode(*merge([part_ref[g.line_from[i], g.c, p], core_recv[i, p]]))
            if d == 0:
                plane_own[i] = state
            else:
                plane_send[i, d - 1] = state.astype(jnp.bfloat16)
                g.go(plane_send.at[i, d - 1], plane_recv.at[i, d - 1],
                     plane_s.at[i, d - 1], plane_r.at[i, d - 1], g.plane(p))

    def reduce_plane(i):
        for d in range(1, PLANE):
            g.arrive(plane_recv.at[i, d - 1], plane_s.at[i, d - 1], plane_r.at[i, d - 1])
        state = encode(*merge([plane_own[i]] + [plane_recv[i, d] for d in range(PLANE - 1)]))
        if i == 0:
            line_own[...] = state
        else:
            line_send[i - 1] = state.astype(jnp.bfloat16)
            g.go(line_send.at[i - 1], line_recv.at[i - 1], line_s.at[i - 1], line_r.at[i - 1],
                 g.line(g.line_from[i]))

    for i in order:
        reduce_core(i)
    for i in order:
        reduce_plane(i)
    for i in range(1, depth):
        g.arrive(line_recv.at[i - 1], line_s.at[i - 1], line_r.at[i - 1])
    numer, _, total = merge([line_own[...]] + [line_recv[i] for i in range(depth - 1)])
    spread[...] = numer / as_column(total)
    for h in range(KVH * GROUP):
        row = 16 * (h // GROUP) + 2 * (h % GROUP)
        out_ref[0, :, h * HEAD : (h + 1) * HEAD] = spread[row : row + 2, :].astype(jnp.bfloat16)
    g.finish()


def body(n, queries, kv_pool, lengths, block_table):
    slots, width = kv_pool.shape[0], block_table.shape[0]
    depth = n // (PLANE * CORES)
    state, bf16, f32, i32 = (ROWS, HEAD), jnp.bfloat16, jnp.float32, jnp.int32
    dma = pltpu.SemaphoreType.DMA
    vmem, anywhere = pl.BlockSpec(memory_space=pltpu.VMEM), pl.BlockSpec(memory_space=pl.ANY)
    far = pl.BlockSpec(memory_space=pltpu.HBM)
    every = jax.ShapeDtypeStruct((depth, CORES, PLANE) + state, bf16)
    meta_shape = (CORES, PLANE, depth, 1, HEAD)

    def params(**more):
        return pltpu.CompilerParams(has_side_effects=True, vmem_limit_bytes=48 * 1024 * 1024, **more)

    every_query, meta = pl.pallas_call(
        functools.partial(gather_kernel, n, width),
        out_shape=[every, jax.ShapeDtypeStruct(meta_shape, i32)],
        in_specs=[far, far, far],
        out_specs=[vmem, vmem],
        scratch_shapes=[
            pltpu.VMEM(state, f32), pltpu.VMEM(queries.shape, bf16),
            pltpu.SMEM((1,), i32), pltpu.SMEM((width,), i32), dma((3,)),
            dma((depth - 1,)), dma((depth - 1,)), dma((PLANE - 1,)), dma((PLANE - 1,)), dma((1,)), dma((1,)),
            dma((depth - 1,)), dma((depth - 1,)), dma((depth, PLANE - 1)), dma((depth, PLANE - 1)),
            dma((depth,)), dma((depth,)),
        ],
        compiler_params=params(collective_id=0),
    )(queries, lengths, block_table)
    parts = pl.pallas_call(
        functools.partial(attend_kernel, n, slots, width),
        out_shape=jax.ShapeDtypeStruct((n,) + state, bf16),
        in_specs=[vmem, anywhere, anywhere],
        out_specs=vmem,
        scratch_shapes=[
            pltpu.VMEM((KVH, slots, BLOCK, 2, HEAD), bf16),
            pltpu.VMEM((2 * BLOCK, HEAD), i32),
            pltpu.SMEM((n, 1, HEAD), i32),
            pltpu.SMEM((width,), i32), pltpu.SMEM((width,), i32), pltpu.SMEM((1,), i32),
            dma((KVH, slots)), dma,
        ],
        compiler_params=params(),
    )(every_query.reshape((n,) + state), meta.reshape(n, 1, HEAD), kv_pool)
    return pl.pallas_call(
        functools.partial(reduce_kernel, n),
        out_shape=jax.ShapeDtypeStruct(queries.shape, queries.dtype),
        in_specs=[vmem],
        out_specs=vmem,
        scratch_shapes=[
            pltpu.VMEM(state, f32),
            pltpu.VMEM((depth, PLANE) + state, bf16),
            pltpu.VMEM((depth, PLANE - 1) + state, bf16),
            pltpu.VMEM((depth, PLANE - 1) + state, bf16),
            pltpu.VMEM((depth,) + state, f32),
            pltpu.VMEM((depth - 1,) + state, bf16),
            pltpu.VMEM((depth - 1,) + state, bf16),
            pltpu.VMEM(state, f32),
            dma((depth,)), dma((depth,)), dma((depth, PLANE - 1)), dma((depth, PLANE - 1)),
            dma((depth - 1,)), dma((depth - 1,)),
        ],
        compiler_params=params(collective_id=1),
    )(parts.reshape(every.shape))


def solution(mesh):
    placed = (P("pool", None, None), P("pool", None, None, None), P("pool"), P("pool"))
    return jax.shard_map(
        functools.partial(body, mesh.shape["pool"]),
        mesh=mesh, in_specs=placed, out_specs=P("pool", None, None), check_vma=False,
    )
```

```python
import functools

import jax
import jax.numpy as jnp
from jax import lax
from jax.experimental import pallas as pl
from jax.experimental.pallas import tpu as pltpu
from jax.sharding import PartitionSpec as P

KVH = 4
GROUP = 7
HEAD = 128
BLOCK = 256
ROWS = 16 * KVH
PLANE = 4
CORES = 2
M_ROW, L_ROW, L_LOW_ROW = 14, 15, 30
MASKED = -1e30
FLOOR = -1e20
UNROLL = 4
SCALE = 1.0 / HEAD**0.5
MESH = pl.DeviceIdType.MESH


def places():
    me = lax.axis_index("pool")
    chip = lax.div(me, CORES)
    z = lax.div(chip, PLANE)
    return me, z, chip - z * PLANE, me - chip * CORES


def wrap(value, size):
    return jnp.where(value >= size, value - size, value)


def remote(src, dst, s, r, to):
    return pltpu.make_async_remote_copy(
        src_ref=src, dst_ref=dst, send_sem=s, recv_sem=r, device_id=to, device_id_type=MESH
    )


def greet(peers):
    barrier = pltpu.get_barrier_semaphore()
    for peer in peers:
        pl.semaphore_signal(barrier, inc=1, device_id=peer, device_id_type=MESH)
    return lambda: pl.semaphore_wait(barrier, len(peers))


class Grid:
    def __init__(self, n):
        self.me, self.z, self.p, self.c = places()
        self.depth = n // (PLANE * CORES)
        self.other = 1 - self.c
        self.line_to = [wrap(self.z + i, self.depth) for i in range(self.depth)]
        self.line_from = [wrap(self.z + self.depth - i, self.depth) for i in range(self.depth)]
        self.plane_to = [wrap(self.p + i, PLANE) for i in range(PLANE)]
        self.plane_from = [wrap(self.p + PLANE - i, PLANE) for i in range(PLANE)]
        self.sent = []

    def at(self, z, p, c):
        return ((z * PLANE + p) * CORES + c,)

    def line(self, z):
        return self.at(z, self.p, self.c)

    def plane(self, p):
        return self.at(self.z, p, self.c)

    def core(self):
        return self.at(self.z, self.p, self.other)

    def peers(self):
        peers = [self.line(z) for z in self.line_to[1:]]
        return peers + [self.plane(p) for p in self.plane_to[1:]] + [self.core()]

    def go(self, src, dst, s, r, to):
        copy = remote(src, dst, s, r, to)
        copy.start()
        self.sent.append(copy)

    def arrive(self, dst, s, r):
        remote(dst, dst, s, r, self.core()).wait_recv()

    def finish(self):
        for copy in self.sent:
            copy.wait_send()


def gather_kernel(
    n, width,
    query_ref, lengths_ref, table_ref, every_query, meta,
    spread, held_query, length_scalar, table_scalar, small_sem,
    meta_line_s, meta_line_r, meta_plane_s, meta_plane_r, meta_core_s, meta_core_r,
    query_line_s, query_line_r, query_plane_s, query_plane_r, query_core_s, query_core_r,
):
    g = Grid(n)
    zz, pp, cc, depth = g.z, g.p, g.c, g.depth
    greeted = greet(g.peers())
    small = [
        pltpu.make_async_copy(lengths_ref, length_scalar, small_sem.at[0]),
        pltpu.make_async_copy(table_ref, table_scalar, small_sem.at[1]),
        pltpu.make_async_copy(query_ref, held_query, small_sem.at[2]),
    ]
    for copy in small:
        copy.start()

    spread[...] = jnp.zeros_like(spread)
    for copy in small:
        copy.wait()
    own_query = held_query[0].astype(jnp.float32)
    for h in range(KVH * GROUP):
        row = 16 * (h // GROUP) + 2 * (h % GROUP)
        spread[row : row + 2, :] = own_query[:, h * HEAD : (h + 1) * HEAD]
    every_query[zz, cc, pp] = spread[...].astype(jnp.bfloat16)
    lane = lax.broadcasted_iota(jnp.int32, (1, HEAD), 1)
    own_meta = jnp.where(lane == width, length_scalar[0], 0)
    for j in range(width):
        own_meta = jnp.where(lane == j, table_scalar[j], own_meta)
    meta[cc, pp, zz] = own_meta
    greeted()

    def query_to_plane(i):
        ref = every_query.at[g.line_from[i], cc, pp]
        for d in range(1, PLANE):
            g.go(ref, ref, query_plane_s.at[i, d - 1], query_plane_r.at[i, d - 1], g.plane(g.plane_to[d]))

    for i in range(1, depth):
        ref = every_query.at[zz, cc, pp]
        g.go(ref, ref, query_line_s.at[i - 1], query_line_r.at[i - 1], g.line(g.line_to[i]))
    for i in range(1, depth):
        ref = meta.at[cc, pp, zz]
        g.go(ref, ref, meta_line_s.at[i - 1], meta_line_r.at[i - 1], g.line(g.line_to[i]))
    query_to_plane(0)
    for i in range(1, depth):
        g.arrive(every_query.at[g.line_from[i], cc, pp], query_line_s.at[i - 1], query_line_r.at[i - 1])
        query_to_plane(i)
    for i in range(1, depth):
        g.arrive(meta.at[cc, pp, g.line_from[i]], meta_line_s.at[i - 1], meta_line_r.at[i - 1])
    for d in range(1, PLANE):
        ref = meta.at[cc, pp]
        g.go(ref, ref, meta_plane_s.at[d - 1], meta_plane_r.at[d - 1], g.plane(g.plane_to[d]))
    for i in range(depth):
        for d in range(1, PLANE):
            g.arrive(every_query.at[g.line_from[i], cc, g.plane_from[d]],
                     query_plane_s.at[i, d - 1], query_plane_r.at[i, d - 1])
        ref = every_query.at[g.line_from[i], cc]
        g.go(ref, ref, query_core_s.at[i], query_core_r.at[i], g.core())
    for d in range(1, PLANE):
        g.arrive(meta.at[cc, g.plane_from[d]], meta_plane_s.at[d - 1], meta_plane_r.at[d - 1])
    ref = meta.at[cc]
    g.go(ref, ref, meta_core_s.at[0], meta_core_r.at[0], g.core())
    for i in range(depth):
        g.arrive(every_query.at[g.line_from[i], g.other], query_core_s.at[i], query_core_r.at[i])
    g.arrive(meta.at[g.other], meta_core_s.at[0], meta_core_r.at[0])
    g.finish()


def state_ids():
    row_id = lax.broadcasted_iota(jnp.int32, (ROWS, HEAD), 0)
    return row_id, row_id == lax.broadcasted_iota(jnp.int32, (ROWS, HEAD), 1)


def encode(numer, peak, total):
    row_id, _ = state_ids()
    high = total.astype(jnp.bfloat16).astype(jnp.float32)
    numer = jnp.where(row_id == M_ROW, peak, numer)
    numer = jnp.where(row_id == L_ROW, high, numer)
    return jnp.where(row_id == L_LOW_ROW, total - high, numer)


def attend_kernel(
    n, slots, width,
    query_ref, meta_ref, pool_ref, out_ref,
    kv, columns, meta_scalar, held_at, held_limit, count_ref, kv_sem, scalar_sem,
):
    me = lax.axis_index("pool")
    stride = n // width
    to_scalar = pltpu.make_async_copy(meta_ref, meta_scalar, scalar_sem)
    to_scalar.start()
    row = lax.broadcasted_iota(jnp.int32, (2 * BLOCK, HEAD), 0)
    lane = lax.broadcasted_iota(jnp.int32, (2 * BLOCK, HEAD), 1)
    columns[...] = jnp.where(row % 2 == 0, row - 2 * (lane % 2), 1 << 24)
    row_id, _ = state_ids()
    empty = jnp.where(row_id == M_ROW, FLOOR, jnp.zeros((ROWS, HEAD), jnp.float32)).astype(out_ref.dtype)
    for request in range(n):
        out_ref[request] = empty
    depth = n // (PLANE * CORES)
    assert (PLANE, CORES) == (4, 2) and slots & (slots - 1) == 0

    def locate(place):
        step = place if stride == 1 else jnp.where(place == 0, 1, place * stride)
        request = me - step
        request = jnp.where(request < 0, request + n, request)
        return request >> 3, (request >> 1) & 3, request & 1

    to_scalar.wait()

    def pool_copies(index, slot):
        return [
            pltpu.make_async_copy(
                pool_ref.at[slot, :, :, pl.ds(k * HEAD, HEAD)], kv.at[k, index], kv_sem.at[k, index]
            )
            for k in range(KVH)
        ]

    count_ref[0] = 0

    @pl.loop(0, width)
    def _(place):
        z, p, c = locate(place)
        line = (c * PLANE + p) * depth + z
        length = meta_scalar[line, 0, width]

        @pl.when(place * BLOCK < length + 2)
        def _():
            index = count_ref[0]
            held_at[index] = (z * CORES + c) * PLANE + p
            held_limit[index] = 2 * (length + 1 - place * BLOCK)
            for copy in pool_copies(index, meta_scalar[line, 0, place] & (slots - 1)):
                copy.start()
            count_ref[0] = index + 1

    count = count_ref[0]
    rows = kv.reshape(KVH, slots, 2 * BLOCK, HEAD)

    lane_row = lax.broadcasted_iota(jnp.int32, (1, HEAD), 1)
    lane_group = lax.broadcasted_iota(jnp.int32, (HEAD, HEAD), 1) // 16

    def attend(indices):
        ats = [held_at[index] for index in indices]
        limit = jnp.where(lane_row < ROWS, held_limit[indices[0]], held_limit[indices[1]])
        pair = jnp.concatenate([query_ref[at] for at in ats], axis=0).astype(jnp.float32)
        pair = jnp.transpose(pair)
        heads = [(r, k) for r in range(2) for k in range(KVH)]
        block = jnp.concatenate([rows[k, indices[r]] for r, k in heads], axis=1)
        query = jnp.concatenate(
            [jnp.where(lane_group == r * KVH + k, pair, 0.0).astype(jnp.bfloat16) for r, k in heads], axis=0
        )
        scores = jnp.dot(block, query, preferred_element_type=jnp.float32)
        scores = jnp.where(columns[...] < limit, scores * SCALE, MASKED)
        peak = jnp.maximum(jnp.max(scores, axis=0, keepdims=True), FLOOR)
        peak = peak.astype(jnp.bfloat16).astype(jnp.float32)
        unscaled = jnp.exp(scores - peak)
        total = jnp.sum(unscaled, axis=0, keepdims=True)
        shifted = pltpu.roll(unscaled.reshape(2 * BLOCK // 8, 8, HEAD), 1, 1).reshape(2 * BLOCK, HEAD)
        weights = jnp.transpose(shifted.astype(jnp.bfloat16))
        states = []
        for r in range(2):
            numers = []
            for k in range(0, KVH, 2):
                block = jnp.concatenate([rows[k, indices[r]], rows[k + 1, indices[r]]], axis=1)
                base = r * ROWS + 16 * k
                both = jnp.dot(weights[base : base + 32], block, preferred_element_type=jnp.float32)
                numers += [both[:16, :HEAD], both[16:, HEAD:]]
            if r == 1:
                peak, total = pltpu.roll(peak, ROWS, 1), pltpu.roll(total, ROWS, 1)
            state = encode(jnp.concatenate(numers, axis=0), peak, total)
            states.append((ats[r], state.astype(out_ref.dtype)))
        return states

    @pl.loop(0, (count + UNROLL - 1) // UNROLL)
    def _(step):
        for u in range(UNROLL):
            index = step * UNROLL + u

            @pl.when(index < count)
            def _():
                for copy in pool_copies(index, 0):
                    copy.wait()

        indices = [jnp.minimum(step * UNROLL + u, count - 1) for u in range(UNROLL)]
        done = [attend(indices[u : u + 2]) for u in range(0, UNROLL, 2)]
        for at, state in sum(done, []):
            out_ref[at] = state


def reduce_kernel(
    n, part_ref, out_ref,
    spread, core_recv, plane_send, plane_recv, plane_own, line_send, line_recv, line_own,
    core_s, core_r, plane_s, plane_r, line_s, line_r,
):
    g = Grid(n)
    depth = g.depth
    greet(g.peers())()
    _, eye = state_ids()

    def as_column(vector):
        return jnp.sum(jnp.where(eye, vector, 0.0), axis=1, keepdims=True)

    def merge(states):
        states = [s.astype(jnp.float32) for s in states]
        peaks = [s[M_ROW : M_ROW + 1] for s in states]
        totals = [s[L_ROW : L_ROW + 1] + s[L_LOW_ROW : L_LOW_ROW + 1] for s in states]
        peak = functools.reduce(jnp.maximum, peaks)
        shrink = [jnp.exp(p - peak) for p in peaks]
        total = sum(a * b for a, b in zip(shrink, totals))
        numer = sum(as_column(a) * s for a, s in zip(shrink, states))
        return numer, peak, total

    order = list(range(1, depth)) + [0]
    for i in order:
        g.go(part_ref.at[g.line_from[i], g.other], core_recv.at[i], core_s.at[i], core_r.at[i], g.core())

    def reduce_core(i):
        g.arrive(core_recv.at[i], core_s.at[i], core_r.at[i])
        states = [
            encode(*merge([part_ref[g.line_from[i], g.c, p], core_recv[i, p]])) for p in g.plane_to
        ]
        plane_own[i] = states[0]
        for d in range(1, PLANE):
            plane_send[i, d - 1] = states[d].astype(jnp.bfloat16)
        for d in range(1, PLANE):
            g.go(plane_send.at[i, d - 1], plane_recv.at[i, d - 1],
                 plane_s.at[i, d - 1], plane_r.at[i, d - 1], g.plane(g.plane_to[d]))

    def reduce_plane(i):
        for d in range(1, PLANE):
            g.arrive(plane_recv.at[i, d - 1], plane_s.at[i, d - 1], plane_r.at[i, d - 1])
        state = encode(*merge([plane_own[i]] + [plane_recv[i, d] for d in range(PLANE - 1)]))
        if i == 0:
            line_own[...] = state
        else:
            line_send[i - 1] = state.astype(jnp.bfloat16)
            g.go(line_send.at[i - 1], line_recv.at[i - 1], line_s.at[i - 1], line_r.at[i - 1],
                 g.line(g.line_from[i]))

    for i in order:
        reduce_core(i)
    for i in order:
        reduce_plane(i)
    for i in range(1, depth):
        g.arrive(line_recv.at[i - 1], line_s.at[i - 1], line_r.at[i - 1])
    numer, _, total = merge([line_own[...]] + [line_recv[i] for i in range(depth - 1)])
    spread[...] = numer / as_column(total)
    for h in range(KVH * GROUP):
        row = 16 * (h // GROUP) + 2 * (h % GROUP)
        out_ref[0, :, h * HEAD : (h + 1) * HEAD] = spread[row : row + 2, :].astype(jnp.bfloat16)
    g.finish()


def body(n, queries, kv_pool, lengths, block_table):
    slots, width = kv_pool.shape[0], block_table.shape[0]
    depth = n // (PLANE * CORES)
    state, bf16, f32, i32 = (ROWS, HEAD), jnp.bfloat16, jnp.float32, jnp.int32
    dma = pltpu.SemaphoreType.DMA
    vmem, anywhere = pl.BlockSpec(memory_space=pltpu.VMEM), pl.BlockSpec(memory_space=pl.ANY)
    far = pl.BlockSpec(memory_space=pltpu.HBM)
    every = jax.ShapeDtypeStruct((depth, CORES, PLANE) + state, bf16)
    meta_shape = (CORES, PLANE, depth, 1, HEAD)

    def params(**more):
        return pltpu.CompilerParams(has_side_effects=True, vmem_limit_bytes=48 * 1024 * 1024, **more)

    every_query, meta = pl.pallas_call(
        functools.partial(gather_kernel, n, width),
        out_shape=[every, jax.ShapeDtypeStruct(meta_shape, i32)],
        in_specs=[far, far, far],
        out_specs=[vmem, vmem],
        scratch_shapes=[
            pltpu.VMEM(state, f32), pltpu.VMEM(queries.shape, bf16),
            pltpu.SMEM((1,), i32), pltpu.SMEM((width,), i32), dma((3,)),
            dma((depth - 1,)), dma((depth - 1,)), dma((PLANE - 1,)), dma((PLANE - 1,)), dma((1,)), dma((1,)),
            dma((depth - 1,)), dma((depth - 1,)), dma((depth, PLANE - 1)), dma((depth, PLANE - 1)),
            dma((depth,)), dma((depth,)),
        ],
        compiler_params=params(collective_id=0),
    )(queries, lengths, block_table)
    parts = pl.pallas_call(
        functools.partial(attend_kernel, n, slots, width),
        out_shape=jax.ShapeDtypeStruct((n,) + state, bf16),
        in_specs=[vmem, anywhere, anywhere],
        out_specs=vmem,
        scratch_shapes=[
            pltpu.VMEM((KVH, slots, BLOCK, 2, HEAD), bf16),
            pltpu.VMEM((2 * BLOCK, HEAD), i32),
            pltpu.SMEM((n, 1, HEAD), i32),
            pltpu.SMEM((width,), i32), pltpu.SMEM((width,), i32), pltpu.SMEM((1,), i32),
            dma((KVH, slots)), dma,
        ],
        compiler_params=params(),
    )(every_query.reshape((n,) + state), meta.reshape(n, 1, HEAD), kv_pool)
    return pl.pallas_call(
        functools.partial(reduce_kernel, n),
        out_shape=jax.ShapeDtypeStruct(queries.shape, queries.dtype),
        in_specs=[vmem],
        out_specs=vmem,
        scratch_shapes=[
            pltpu.VMEM(state, f32),
            pltpu.VMEM((depth, PLANE) + state, bf16),
            pltpu.VMEM((depth, PLANE - 1) + state, bf16),
            pltpu.VMEM((depth, PLANE - 1) + state, bf16),
            pltpu.VMEM((depth,) + state, f32),
            pltpu.VMEM((depth - 1,) + state, bf16),
            pltpu.VMEM((depth - 1,) + state, bf16),
            pltpu.VMEM(state, f32),
            dma((depth,)), dma((depth,)), dma((depth, PLANE - 1)), dma((depth, PLANE - 1)),
            dma((depth - 1,)), dma((depth - 1,)),
        ],
        compiler_params=params(collective_id=1),
    )(parts.reshape(every.shape))


def solution(mesh):
    placed = (P("pool", None, None), P("pool", None, None, None), P("pool"), P("pool"))
    return jax.shard_map(
        functools.partial(body, mesh.shape["pool"]),
        mesh=mesh, in_specs=placed, out_specs=P("pool", None, None), check_vma=False,
    )
```

```python
import functools

import jax
import jax.numpy as jnp
from jax import lax
from jax.experimental import pallas as pl
from jax.experimental.pallas import tpu as pltpu
from jax.sharding import PartitionSpec as P

KVH = 4
GROUP = 7
HEAD = 128
BLOCK = 256
ROWS = 16 * KVH
PLANE = 4
CORES = 2
M_ROW, L_ROW, L_LOW_ROW = 14, 15, 30
MASKED = -1e30
FLOOR = -1e20
UNROLL = 4
KV_CHUNKS = 4
SCALE = 1.0 / HEAD**0.5
MESH = pl.DeviceIdType.MESH


def places():
    me = lax.axis_index("pool")
    chip = lax.div(me, CORES)
    z = lax.div(chip, PLANE)
    return me, z, chip - z * PLANE, me - chip * CORES


def wrap(value, size):
    return jnp.where(value >= size, value - size, value)


def remote(src, dst, s, r, to):
    return pltpu.make_async_remote_copy(
        src_ref=src, dst_ref=dst, send_sem=s, recv_sem=r, device_id=to, device_id_type=MESH
    )


def greet(peers):
    barrier = pltpu.get_barrier_semaphore()
    for peer in peers:
        pl.semaphore_signal(barrier, inc=1, device_id=peer, device_id_type=MESH)
    return lambda: pl.semaphore_wait(barrier, len(peers))


class Grid:
    def __init__(self, n):
        self.me, self.z, self.p, self.c = places()
        self.depth = n // (PLANE * CORES)
        self.other = 1 - self.c
        self.line_to = [wrap(self.z + i, self.depth) for i in range(self.depth)]
        self.line_from = [wrap(self.z + self.depth - i, self.depth) for i in range(self.depth)]
        self.plane_to = [wrap(self.p + i, PLANE) for i in range(PLANE)]
        self.plane_from = [wrap(self.p + PLANE - i, PLANE) for i in range(PLANE)]
        self.sent = []

    def at(self, z, p, c):
        return ((z * PLANE + p) * CORES + c,)

    def line(self, z):
        return self.at(z, self.p, self.c)

    def plane(self, p):
        return self.at(self.z, p, self.c)

    def core(self):
        return self.at(self.z, self.p, self.other)

    def peers(self):
        peers = [self.line(z) for z in self.line_to[1:]]
        return peers + [self.plane(p) for p in self.plane_to[1:]] + [self.core()]

    def go(self, src, dst, s, r, to):
        copy = remote(src, dst, s, r, to)
        copy.start()
        self.sent.append(copy)

    def arrive(self, dst, s, r):
        remote(dst, dst, s, r, self.core()).wait_recv()

    def finish(self):
        for copy in self.sent:
            copy.wait_send()


def gather_kernel(
    n, slots, width,
    query_ref, lengths_ref, table_ref, pool_ref, every_query, meta, kv,
    spread, held_query, length_scalar, table_scalar, small_sem, kv_sem,
    meta_line_s, meta_line_r, meta_plane_s, meta_plane_r, meta_core_s, meta_core_r,
    query_line_s, query_line_r, query_plane_s, query_plane_r, query_core_s, query_core_r,
):
    g = Grid(n)
    zz, pp, cc, depth = g.z, g.p, g.c, g.depth
    greeted = greet(g.peers())
    chunk = slots // KV_CHUNKS
    kv_copies = [
        pltpu.make_async_copy(
            pool_ref.at[pl.ds(part * chunk, chunk), :, :, pl.ds(k * HEAD, HEAD)],
            kv.at[k, pl.ds(part * chunk, chunk)],
            kv_sem.at[part, k],
        )
        for part in range(KV_CHUNKS)
        for k in range(KVH)
    ]
    small = [
        pltpu.make_async_copy(lengths_ref, length_scalar, small_sem.at[0]),
        pltpu.make_async_copy(table_ref, table_scalar, small_sem.at[1]),
        pltpu.make_async_copy(query_ref, held_query, small_sem.at[2]),
    ]
    for copy in small + kv_copies:
        copy.start()

    spread[...] = jnp.zeros_like(spread)
    for copy in small:
        copy.wait()
    own_query = held_query[0].astype(jnp.float32)
    for h in range(KVH * GROUP):
        row = 16 * (h // GROUP) + 2 * (h % GROUP)
        spread[row : row + 2, :] = own_query[:, h * HEAD : (h + 1) * HEAD]
    every_query[zz, cc, pp] = spread[...].astype(jnp.bfloat16)
    lane = lax.broadcasted_iota(jnp.int32, (1, HEAD), 1)
    own_meta = jnp.where(lane == width, length_scalar[0], 0)
    for j in range(width):
        own_meta = jnp.where(lane == j, table_scalar[j], own_meta)
    meta[cc, pp, zz] = own_meta
    greeted()

    def query_to_plane(i):
        ref = every_query.at[g.line_from[i], cc, pp]
        for d in range(1, PLANE):
            g.go(ref, ref, query_plane_s.at[i, d - 1], query_plane_r.at[i, d - 1], g.plane(g.plane_to[d]))

    for i in range(1, depth):
        ref = every_query.at[zz, cc, pp]
        g.go(ref, ref, query_line_s.at[i - 1], query_line_r.at[i - 1], g.line(g.line_to[i]))
    for i in range(1, depth):
        ref = meta.at[cc, pp, zz]
        g.go(ref, ref, meta_line_s.at[i - 1], meta_line_r.at[i - 1], g.line(g.line_to[i]))
    query_to_plane(0)
    for i in range(1, depth):
        g.arrive(every_query.at[g.line_from[i], cc, pp], query_line_s.at[i - 1], query_line_r.at[i - 1])
        query_to_plane(i)
    for i in range(1, depth):
        g.arrive(meta.at[cc, pp, g.line_from[i]], meta_line_s.at[i - 1], meta_line_r.at[i - 1])
    for d in range(1, PLANE):
        ref = meta.at[cc, pp]
        g.go(ref, ref, meta_plane_s.at[d - 1], meta_plane_r.at[d - 1], g.plane(g.plane_to[d]))
    for i in range(depth):
        for d in range(1, PLANE):
            g.arrive(every_query.at[g.line_from[i], cc, g.plane_from[d]],
                     query_plane_s.at[i, d - 1], query_plane_r.at[i, d - 1])
        ref = every_query.at[g.line_from[i], cc]
        g.go(ref, ref, query_core_s.at[i], query_core_r.at[i], g.core())
    for d in range(1, PLANE):
        g.arrive(meta.at[cc, g.plane_from[d]], meta_plane_s.at[d - 1], meta_plane_r.at[d - 1])
    ref = meta.at[cc]
    g.go(ref, ref, meta_core_s.at[0], meta_core_r.at[0], g.core())
    for i in range(depth):
        g.arrive(every_query.at[g.line_from[i], g.other], query_core_s.at[i], query_core_r.at[i])
    g.arrive(meta.at[g.other], meta_core_s.at[0], meta_core_r.at[0])
    g.finish()
    for copy in kv_copies:
        copy.wait()


def state_ids():
    row_id = lax.broadcasted_iota(jnp.int32, (ROWS, HEAD), 0)
    return row_id, row_id == lax.broadcasted_iota(jnp.int32, (ROWS, HEAD), 1)


def encode(numer, peak, total):
    row_id, _ = state_ids()
    high = total.astype(jnp.bfloat16).astype(jnp.float32)
    numer = jnp.where(row_id == M_ROW, peak, numer)
    numer = jnp.where(row_id == L_ROW, high, numer)
    return jnp.where(row_id == L_LOW_ROW, total - high, numer)


def attend_kernel(
    n, slots, width,
    query_ref, meta_ref, kv, out_ref,
    columns, meta_scalar, held_at, held_slot, held_limit, count_ref, scalar_sem,
):
    me = lax.axis_index("pool")
    stride = n // width
    to_scalar = pltpu.make_async_copy(meta_ref, meta_scalar, scalar_sem)
    to_scalar.start()
    row = lax.broadcasted_iota(jnp.int32, (2 * BLOCK, HEAD), 0)
    lane = lax.broadcasted_iota(jnp.int32, (2 * BLOCK, HEAD), 1)
    columns[...] = jnp.where(row % 2 == 0, row - 2 * (lane % 2), 1 << 24)
    row_id, _ = state_ids()
    empty = jnp.where(row_id == M_ROW, FLOOR, jnp.zeros((ROWS, HEAD), jnp.float32)).astype(out_ref.dtype)
    for request in range(n):
        out_ref[request] = empty
    depth = n // (PLANE * CORES)
    assert (PLANE, CORES) == (4, 2) and slots & (slots - 1) == 0

    def locate(place):
        step = place if stride == 1 else jnp.where(place == 0, 1, place * stride)
        request = me - step
        request = jnp.where(request < 0, request + n, request)
        return request >> 3, (request >> 1) & 3, request & 1

    to_scalar.wait()

    count_ref[0] = 0

    @pl.loop(0, width)
    def _(place):
        z, p, c = locate(place)
        line = (c * PLANE + p) * depth + z
        length = meta_scalar[line, 0, width]

        @pl.when(place * BLOCK < length + 2)
        def _():
            index = count_ref[0]
            held_at[index] = (z * CORES + c) * PLANE + p
            held_limit[index] = 2 * (length + 1 - place * BLOCK)
            held_slot[index] = meta_scalar[line, 0, place] & (slots - 1)
            count_ref[0] = index + 1

    count = count_ref[0]
    rows = kv.reshape(KVH, slots, 2 * BLOCK, HEAD)

    lane_row = lax.broadcasted_iota(jnp.int32, (1, HEAD), 1)
    lane_group = lax.broadcasted_iota(jnp.int32, (HEAD, HEAD), 1) // 16

    def attend(indices):
        ats = [held_at[index] for index in indices]
        held = [held_slot[index] for index in indices]
        limit = jnp.where(lane_row < ROWS, held_limit[indices[0]], held_limit[indices[1]])
        pair = jnp.concatenate([query_ref[at] for at in ats], axis=0).astype(jnp.float32)
        pair = jnp.transpose(pair)
        heads = [(r, k) for r in range(2) for k in range(KVH)]
        block = jnp.concatenate([rows[k, held[r]] for r, k in heads], axis=1)
        query = jnp.concatenate(
            [jnp.where(lane_group == r * KVH + k, pair, 0.0).astype(jnp.bfloat16) for r, k in heads], axis=0
        )
        scores = jnp.dot(block, query, preferred_element_type=jnp.float32)
        scores = jnp.where(columns[...] < limit, scores * SCALE, MASKED)
        peak = jnp.maximum(jnp.max(scores, axis=0, keepdims=True), FLOOR)
        peak = peak.astype(jnp.bfloat16).astype(jnp.float32)
        unscaled = jnp.exp(scores - peak)
        total = jnp.sum(unscaled, axis=0, keepdims=True)
        shifted = pltpu.roll(unscaled.reshape(2 * BLOCK // 8, 8, HEAD), 1, 1).reshape(2 * BLOCK, HEAD)
        weights = jnp.transpose(shifted.astype(jnp.bfloat16))
        states = []
        for r in range(2):
            numers = []
            for k in range(0, KVH, 2):
                block = jnp.concatenate([rows[k, held[r]], rows[k + 1, held[r]]], axis=1)
                base = r * ROWS + 16 * k
                both = jnp.dot(weights[base : base + 32], block, preferred_element_type=jnp.float32)
                numers += [both[:16, :HEAD], both[16:, HEAD:]]
            if r == 1:
                peak, total = pltpu.roll(peak, ROWS, 1), pltpu.roll(total, ROWS, 1)
            state = encode(jnp.concatenate(numers, axis=0), peak, total)
            states.append((ats[r], state.astype(out_ref.dtype)))
        return states

    @pl.loop(0, (count + UNROLL - 1) // UNROLL)
    def _(step):
        indices = [jnp.minimum(step * UNROLL + u, count - 1) for u in range(UNROLL)]
        done = [attend(indices[u : u + 2]) for u in range(0, UNROLL, 2)]
        for at, state in sum(done, []):
            out_ref[at] = state


def reduce_kernel(
    n, part_ref, out_ref,
    spread, core_recv, plane_send, plane_recv, plane_own, line_send, line_recv, line_own,
    core_s, core_r, plane_s, plane_r, line_s, line_r,
):
    g = Grid(n)
    depth = g.depth
    greet(g.peers())()
    _, eye = state_ids()

    def as_column(vector):
        return jnp.sum(jnp.where(eye, vector, 0.0), axis=1, keepdims=True)

    def merge(states):
        states = [s.astype(jnp.float32) for s in states]
        peaks = [s[M_ROW : M_ROW + 1] for s in states]
        totals = [s[L_ROW : L_ROW + 1] + s[L_LOW_ROW : L_LOW_ROW + 1] for s in states]
        peak = functools.reduce(jnp.maximum, peaks)
        shrink = [jnp.exp(p - peak) for p in peaks]
        total = sum(a * b for a, b in zip(shrink, totals))
        numer = sum(as_column(a) * s for a, s in zip(shrink, states))
        return numer, peak, total

    order = list(range(1, depth)) + [0]
    for i in order:
        g.go(part_ref.at[g.line_from[i], g.other], core_recv.at[i], core_s.at[i], core_r.at[i], g.core())

    def reduce_core(i):
        g.arrive(core_recv.at[i], core_s.at[i], core_r.at[i])
        states = [
            encode(*merge([part_ref[g.line_from[i], g.c, p], core_recv[i, p]])) for p in g.plane_to
        ]
        plane_own[i] = states[0]
        for d in range(1, PLANE):
            plane_send[i, d - 1] = states[d].astype(jnp.bfloat16)
        for d in range(1, PLANE):
            g.go(plane_send.at[i, d - 1], plane_recv.at[i, d - 1],
                 plane_s.at[i, d - 1], plane_r.at[i, d - 1], g.plane(g.plane_to[d]))

    def reduce_plane(i):
        for d in range(1, PLANE):
            g.arrive(plane_recv.at[i, d - 1], plane_s.at[i, d - 1], plane_r.at[i, d - 1])
        state = encode(*merge([plane_own[i]] + [plane_recv[i, d] for d in range(PLANE - 1)]))
        if i == 0:
            line_own[...] = state
        else:
            line_send[i - 1] = state.astype(jnp.bfloat16)
            g.go(line_send.at[i - 1], line_recv.at[i - 1], line_s.at[i - 1], line_r.at[i - 1],
                 g.line(g.line_from[i]))

    for i in order:
        reduce_core(i)
    for i in order:
        reduce_plane(i)
    for i in range(1, depth):
        g.arrive(line_recv.at[i - 1], line_s.at[i - 1], line_r.at[i - 1])
    numer, _, total = merge([line_own[...]] + [line_recv[i] for i in range(depth - 1)])
    spread[...] = numer / as_column(total)
    for h in range(KVH * GROUP):
        row = 16 * (h // GROUP) + 2 * (h % GROUP)
        out_ref[0, :, h * HEAD : (h + 1) * HEAD] = spread[row : row + 2, :].astype(jnp.bfloat16)
    g.finish()


def body(n, queries, kv_pool, lengths, block_table):
    slots, width = kv_pool.shape[0], block_table.shape[0]
    depth = n // (PLANE * CORES)
    state, bf16, f32, i32 = (ROWS, HEAD), jnp.bfloat16, jnp.float32, jnp.int32
    dma = pltpu.SemaphoreType.DMA
    vmem, anywhere = pl.BlockSpec(memory_space=pltpu.VMEM), pl.BlockSpec(memory_space=pl.ANY)
    far = pl.BlockSpec(memory_space=pltpu.HBM)
    every = jax.ShapeDtypeStruct((depth, CORES, PLANE) + state, bf16)
    meta_shape = (CORES, PLANE, depth, 1, HEAD)

    def params(**more):
        return pltpu.CompilerParams(has_side_effects=True, vmem_limit_bytes=28 * 1024 * 1024, **more)

    every_query, meta, kv = pl.pallas_call(
        functools.partial(gather_kernel, n, slots, width),
        out_shape=[
            every,
            jax.ShapeDtypeStruct(meta_shape, i32),
            jax.ShapeDtypeStruct((KVH, slots, BLOCK, 2, HEAD), bf16),
        ],
        in_specs=[far, far, far, anywhere],
        out_specs=[vmem, vmem, vmem],
        scratch_shapes=[
            pltpu.VMEM(state, f32), pltpu.VMEM(queries.shape, bf16),
            pltpu.SMEM((1,), i32), pltpu.SMEM((width,), i32), dma((3,)), dma((KV_CHUNKS, KVH)),
            dma((depth - 1,)), dma((depth - 1,)), dma((PLANE - 1,)), dma((PLANE - 1,)), dma((1,)), dma((1,)),
            dma((depth - 1,)), dma((depth - 1,)), dma((depth, PLANE - 1)), dma((depth, PLANE - 1)),
            dma((depth,)), dma((depth,)),
        ],
        compiler_params=params(collective_id=0),
    )(queries, lengths, block_table, kv_pool)
    parts = pl.pallas_call(
        functools.partial(attend_kernel, n, slots, width),
        out_shape=jax.ShapeDtypeStruct((n,) + state, bf16),
        in_specs=[vmem, anywhere, vmem],
        out_specs=vmem,
        scratch_shapes=[
            pltpu.VMEM((2 * BLOCK, HEAD), i32),
            pltpu.SMEM((n, 1, HEAD), i32),
            pltpu.SMEM((width,), i32), pltpu.SMEM((width,), i32), pltpu.SMEM((width,), i32),
            pltpu.SMEM((1,), i32), dma,
        ],
        compiler_params=params(),
    )(every_query.reshape((n,) + state), meta.reshape(n, 1, HEAD), kv)
    return pl.pallas_call(
        functools.partial(reduce_kernel, n),
        out_shape=jax.ShapeDtypeStruct(queries.shape, queries.dtype),
        in_specs=[vmem],
        out_specs=vmem,
        scratch_shapes=[
            pltpu.VMEM(state, f32),
            pltpu.VMEM((depth, PLANE) + state, bf16),
            pltpu.VMEM((depth, PLANE - 1) + state, bf16),
            pltpu.VMEM((depth, PLANE - 1) + state, bf16),
            pltpu.VMEM((depth,) + state, f32),
            pltpu.VMEM((depth - 1,) + state, bf16),
            pltpu.VMEM((depth - 1,) + state, bf16),
            pltpu.VMEM(state, f32),
            dma((depth,)), dma((depth,)), dma((depth, PLANE - 1)), dma((depth, PLANE - 1)),
            dma((depth - 1,)), dma((depth - 1,)),
        ],
        compiler_params=params(collective_id=1),
    )(parts.reshape(every.shape))


def solution(mesh):
    placed = (P("pool", None, None), P("pool", None, None, None), P("pool"), P("pool"))
    return jax.shard_map(
        functools.partial(body, mesh.shape["pool"]),
        mesh=mesh, in_specs=placed, out_specs=P("pool", None, None), check_vma=False,
    )
```

```python
import functools

import jax
import jax.numpy as jnp
from jax import lax
from jax.experimental import pallas as pl
from jax.experimental.pallas import tpu as pltpu
from jax.sharding import PartitionSpec as P

KVH = 4
GROUP = 7
HEAD = 128
BLOCK = 256
ROWS = 16 * KVH
PLANE = 4
CORES = 2
M_ROW, L_ROW, L_LOW_ROW = 14, 15, 30
MASKED = -1e30
FLOOR = -1e20
UNROLL = 2
KV_CHUNKS = 4
SCALE = 1.0 / HEAD**0.5
MESH = pl.DeviceIdType.MESH


def places():
    me = lax.axis_index("pool")
    chip = lax.div(me, CORES)
    z = lax.div(chip, PLANE)
    return me, z, chip - z * PLANE, me - chip * CORES


def wrap(value, size):
    return jnp.where(value >= size, value - size, value)


def remote(src, dst, s, r, to):
    return pltpu.make_async_remote_copy(
        src_ref=src, dst_ref=dst, send_sem=s, recv_sem=r, device_id=to, device_id_type=MESH
    )


def greet(peers):
    barrier = pltpu.get_barrier_semaphore()
    for peer in peers:
        pl.semaphore_signal(barrier, inc=1, device_id=peer, device_id_type=MESH)
    return lambda: pl.semaphore_wait(barrier, len(peers))


class Grid:
    def __init__(self, n):
        self.me, self.z, self.p, self.c = places()
        self.depth = n // (PLANE * CORES)
        self.other = 1 - self.c
        self.line_to = [wrap(self.z + i, self.depth) for i in range(self.depth)]
        self.line_from = [wrap(self.z + self.depth - i, self.depth) for i in range(self.depth)]
        self.plane_to = [wrap(self.p + i, PLANE) for i in range(PLANE)]
        self.plane_from = [wrap(self.p + PLANE - i, PLANE) for i in range(PLANE)]
        self.sent = []

    def at(self, z, p, c):
        return ((z * PLANE + p) * CORES + c,)

    def line(self, z):
        return self.at(z, self.p, self.c)

    def plane(self, p):
        return self.at(self.z, p, self.c)

    def core(self):
        return self.at(self.z, self.p, self.other)

    def peers(self):
        peers = [self.line(z) for z in self.line_to[1:]]
        return peers + [self.plane(p) for p in self.plane_to[1:]] + [self.core()]

    def go(self, src, dst, s, r, to):
        copy = remote(src, dst, s, r, to)
        copy.start()
        self.sent.append(copy)

    def arrive(self, dst, s, r):
        remote(dst, dst, s, r, self.core()).wait_recv()

    def finish(self):
        for copy in self.sent:
            copy.wait_send()


def gather_kernel(
    n, slots, width,
    query_ref, lengths_ref, table_ref, pool_ref, every_query, meta, kv,
    spread, held_query, length_scalar, table_scalar, small_sem, kv_sem,
    meta_line_s, meta_line_r, meta_plane_s, meta_plane_r, meta_core_s, meta_core_r,
    query_line_s, query_line_r, query_plane_s, query_plane_r, query_core_s, query_core_r,
):
    g = Grid(n)
    zz, pp, cc, depth = g.z, g.p, g.c, g.depth
    greeted = greet(g.peers())
    chunk = slots // KV_CHUNKS
    kv_copies = [
        pltpu.make_async_copy(
            pool_ref.at[pl.ds(part * chunk, chunk), :, :, pl.ds(k * HEAD, HEAD)],
            kv.at[k, pl.ds(part * chunk, chunk)],
            kv_sem.at[part, k],
        )
        for part in range(KV_CHUNKS)
        for k in range(KVH)
    ]
    small = [
        pltpu.make_async_copy(lengths_ref, length_scalar, small_sem.at[0]),
        pltpu.make_async_copy(table_ref, table_scalar, small_sem.at[1]),
        pltpu.make_async_copy(query_ref, held_query, small_sem.at[2]),
    ]
    for copy in small + kv_copies:
        copy.start()

    spread[...] = jnp.zeros_like(spread)
    for copy in small:
        copy.wait()
    own_query = held_query[0].astype(jnp.float32)
    for h in range(KVH * GROUP):
        row = 16 * (h // GROUP) + 2 * (h % GROUP)
        spread[row : row + 2, :] = own_query[:, h * HEAD : (h + 1) * HEAD]
    every_query[zz, cc, pp] = spread[...].astype(jnp.bfloat16)
    lane = lax.broadcasted_iota(jnp.int32, (1, HEAD), 1)
    own_meta = jnp.where(lane == width, length_scalar[0], 0)
    for j in range(width):
        own_meta = jnp.where(lane == j, table_scalar[j], own_meta)
    meta[cc, pp, zz] = own_meta
    greeted()

    def query_to_plane(i):
        ref = every_query.at[g.line_from[i], cc, pp]
        for d in range(1, PLANE):
            g.go(ref, ref, query_plane_s.at[i, d - 1], query_plane_r.at[i, d - 1], g.plane(g.plane_to[d]))

    for i in range(1, depth):
        ref = every_query.at[zz, cc, pp]
        g.go(ref, ref, query_line_s.at[i - 1], query_line_r.at[i - 1], g.line(g.line_to[i]))
    for i in range(1, depth):
        ref = meta.at[cc, pp, zz]
        g.go(ref, ref, meta_line_s.at[i - 1], meta_line_r.at[i - 1], g.line(g.line_to[i]))
    query_to_plane(0)
    for i in range(1, depth):
        g.arrive(every_query.at[g.line_from[i], cc, pp], query_line_s.at[i - 1], query_line_r.at[i - 1])
        query_to_plane(i)
    for i in range(1, depth):
        g.arrive(meta.at[cc, pp, g.line_from[i]], meta_line_s.at[i - 1], meta_line_r.at[i - 1])
    for d in range(1, PLANE):
        ref = meta.at[cc, pp]
        g.go(ref, ref, meta_plane_s.at[d - 1], meta_plane_r.at[d - 1], g.plane(g.plane_to[d]))
    for i in range(depth):
        for d in range(1, PLANE):
            g.arrive(every_query.at[g.line_from[i], cc, g.plane_from[d]],
                     query_plane_s.at[i, d - 1], query_plane_r.at[i, d - 1])
        ref = every_query.at[g.line_from[i], cc]
        g.go(ref, ref, query_core_s.at[i], query_core_r.at[i], g.core())
    for d in range(1, PLANE):
        g.arrive(meta.at[cc, g.plane_from[d]], meta_plane_s.at[d - 1], meta_plane_r.at[d - 1])
    ref = meta.at[cc]
    g.go(ref, ref, meta_core_s.at[0], meta_core_r.at[0], g.core())
    for i in range(depth):
        g.arrive(every_query.at[g.line_from[i], g.other], query_core_s.at[i], query_core_r.at[i])
    g.arrive(meta.at[g.other], meta_core_s.at[0], meta_core_r.at[0])
    g.finish()
    for copy in kv_copies:
        copy.wait()


def state_ids():
    row_id = lax.broadcasted_iota(jnp.int32, (ROWS, HEAD), 0)
    return row_id, row_id == lax.broadcasted_iota(jnp.int32, (ROWS, HEAD), 1)


def encode(numer, peak, total):
    row_id, _ = state_ids()
    high = total.astype(jnp.bfloat16).astype(jnp.float32)
    numer = jnp.where(row_id == M_ROW, peak, numer)
    numer = jnp.where(row_id == L_ROW, high, numer)
    return jnp.where(row_id == L_LOW_ROW, total - high, numer)


def attend_kernel(
    n, slots, width,
    query_ref, meta_ref, kv, out_ref,
    columns, meta_scalar, held_at, held_slot, held_limit, count_ref, scalar_sem,
):
    me = lax.axis_index("pool")
    stride = n // width
    to_scalar = pltpu.make_async_copy(meta_ref, meta_scalar, scalar_sem)
    to_scalar.start()
    row = lax.broadcasted_iota(jnp.int32, (2 * BLOCK, HEAD), 0)
    lane = lax.broadcasted_iota(jnp.int32, (2 * BLOCK, HEAD), 1)
    columns[...] = jnp.where(row % 2 == 0, row - 2 * (lane % 2), 1 << 24)
    row_id, _ = state_ids()
    empty = jnp.where(row_id == M_ROW, FLOOR, jnp.zeros((ROWS, HEAD), jnp.float32)).astype(out_ref.dtype)
    for request in range(n):
        out_ref[request] = empty
    depth = n // (PLANE * CORES)
    assert (PLANE, CORES) == (4, 2) and slots & (slots - 1) == 0

    def locate(place):
        step = place if stride == 1 else jnp.where(place == 0, 1, place * stride)
        request = me - step
        request = jnp.where(request < 0, request + n, request)
        return request >> 3, (request >> 1) & 3, request & 1

    to_scalar.wait()

    count_ref[0] = 0

    @pl.loop(0, width)
    def _(place):
        z, p, c = locate(place)
        line = (c * PLANE + p) * depth + z
        length = meta_scalar[line, 0, width]

        @pl.when(place * BLOCK < length + 2)
        def _():
            index = count_ref[0]
            held_at[index] = (z * CORES + c) * PLANE + p
            held_limit[index] = 2 * (length + 1 - place * BLOCK)
            held_slot[index] = meta_scalar[line, 0, place] & (slots - 1)
            count_ref[0] = index + 1

    count = count_ref[0]
    rows = kv.reshape(KVH, slots, 2 * BLOCK, HEAD)

    lane_row = lax.broadcasted_iota(jnp.int32, (1, HEAD), 1)
    lane_group = lax.broadcasted_iota(jnp.int32, (HEAD, HEAD), 1) // 16

    def attend(indices):
        ats = [held_at[index] for index in indices]
        held = [held_slot[index] for index in indices]
        limit = jnp.where(lane_row < ROWS, held_limit[indices[0]], held_limit[indices[1]])
        pair = jnp.concatenate([query_ref[at] for at in ats], axis=0).astype(jnp.float32)
        pair = jnp.transpose(pair)
        heads = [(r, k) for r in range(2) for k in range(KVH)]
        block = jnp.concatenate([rows[k, held[r]] for r, k in heads], axis=1)
        query = jnp.concatenate(
            [jnp.where(lane_group == r * KVH + k, pair, 0.0).astype(jnp.bfloat16) for r, k in heads], axis=0
        )
        scores = jnp.dot(block, query, preferred_element_type=jnp.float32)
        scores = jnp.where(columns[...] < limit, scores * SCALE, MASKED)
        peak = jnp.maximum(jnp.max(scores, axis=0, keepdims=True), FLOOR)
        peak = peak.astype(jnp.bfloat16).astype(jnp.float32)
        unscaled = jnp.exp(scores - peak)
        total = jnp.sum(unscaled, axis=0, keepdims=True)
        shifted = pltpu.roll(unscaled.reshape(2 * BLOCK // 8, 8, HEAD), 1, 1).reshape(2 * BLOCK, HEAD)
        weights = jnp.transpose(shifted.astype(jnp.bfloat16))
        states = []
        for r in range(2):
            numers = []
            for k in range(0, KVH, 2):
                block = jnp.concatenate([rows[k, held[r]], rows[k + 1, held[r]]], axis=1)
                base = r * ROWS + 16 * k
                both = jnp.dot(weights[base : base + 32], block, preferred_element_type=jnp.float32)
                numers += [both[:16, :HEAD], both[16:, HEAD:]]
            if r == 1:
                peak, total = pltpu.roll(peak, ROWS, 1), pltpu.roll(total, ROWS, 1)
            state = encode(jnp.concatenate(numers, axis=0), peak, total)
            states.append((ats[r], state.astype(out_ref.dtype)))
        return states

    @pl.loop(0, (count + UNROLL - 1) // UNROLL)
    def _(step):
        indices = [jnp.minimum(step * UNROLL + u, count - 1) for u in range(UNROLL)]
        done = [attend(indices[u : u + 2]) for u in range(0, UNROLL, 2)]
        for at, state in sum(done, []):
            out_ref[at] = state


def reduce_kernel(
    n, part_ref, out_ref,
    spread, core_recv, plane_send, plane_recv, plane_own, line_send, line_recv, line_own,
    core_s, core_r, plane_s, plane_r, line_s, line_r,
):
    g = Grid(n)
    depth = g.depth
    greet(g.peers())()
    _, eye = state_ids()

    def as_column(vector):
        return jnp.sum(jnp.where(eye, vector, 0.0), axis=1, keepdims=True)

    def merge(states):
        states = [s.astype(jnp.float32) for s in states]
        peaks = [s[M_ROW : M_ROW + 1] for s in states]
        totals = [s[L_ROW : L_ROW + 1] + s[L_LOW_ROW : L_LOW_ROW + 1] for s in states]
        peak = functools.reduce(jnp.maximum, peaks)
        shrink = [jnp.exp(p - peak) for p in peaks]
        total = sum(a * b for a, b in zip(shrink, totals))
        numer = sum(as_column(a) * s for a, s in zip(shrink, states))
        return numer, peak, total

    order = list(range(1, depth)) + [0]
    for i in order:
        g.go(part_ref.at[g.line_from[i], g.other], core_recv.at[i], core_s.at[i], core_r.at[i], g.core())

    def reduce_core(i):
        g.arrive(core_recv.at[i], core_s.at[i], core_r.at[i])
        states = [
            encode(*merge([part_ref[g.line_from[i], g.c, p], core_recv[i, p]])) for p in g.plane_to
        ]
        plane_own[i] = states[0]
        for d in range(1, PLANE):
            plane_send[i, d - 1] = states[d].astype(jnp.bfloat16)
        for d in range(1, PLANE):
            g.go(plane_send.at[i, d - 1], plane_recv.at[i, d - 1],
                 plane_s.at[i, d - 1], plane_r.at[i, d - 1], g.plane(g.plane_to[d]))

    def reduce_plane(i):
        for d in range(1, PLANE):
            g.arrive(plane_recv.at[i, d - 1], plane_s.at[i, d - 1], plane_r.at[i, d - 1])
        state = encode(*merge([plane_own[i]] + [plane_recv[i, d] for d in range(PLANE - 1)]))
        if i == 0:
            line_own[...] = state
        else:
            line_send[i - 1] = state.astype(jnp.bfloat16)
            g.go(line_send.at[i - 1], line_recv.at[i - 1], line_s.at[i - 1], line_r.at[i - 1],
                 g.line(g.line_from[i]))

    for i in order:
        reduce_core(i)
    for i in order:
        reduce_plane(i)
    for i in range(1, depth):
        g.arrive(line_recv.at[i - 1], line_s.at[i - 1], line_r.at[i - 1])
    numer, _, total = merge([line_own[...]] + [line_recv[i] for i in range(depth - 1)])
    spread[...] = numer / as_column(total)
    for h in range(KVH * GROUP):
        row = 16 * (h // GROUP) + 2 * (h % GROUP)
        out_ref[0, :, h * HEAD : (h + 1) * HEAD] = spread[row : row + 2, :].astype(jnp.bfloat16)
    g.finish()


def body(n, queries, kv_pool, lengths, block_table):
    slots, width = kv_pool.shape[0], block_table.shape[0]
    depth = n // (PLANE * CORES)
    state, bf16, f32, i32 = (ROWS, HEAD), jnp.bfloat16, jnp.float32, jnp.int32
    dma = pltpu.SemaphoreType.DMA
    vmem, anywhere = pl.BlockSpec(memory_space=pltpu.VMEM), pl.BlockSpec(memory_space=pl.ANY)
    far = pl.BlockSpec(memory_space=pltpu.HBM)
    every = jax.ShapeDtypeStruct((depth, CORES, PLANE) + state, bf16)
    meta_shape = (CORES, PLANE, depth, 1, HEAD)

    def params(**more):
        return pltpu.CompilerParams(has_side_effects=True, vmem_limit_bytes=28 * 1024 * 1024, **more)

    every_query, meta, kv = pl.pallas_call(
        functools.partial(gather_kernel, n, slots, width),
        out_shape=[
            every,
            jax.ShapeDtypeStruct(meta_shape, i32),
            jax.ShapeDtypeStruct((KVH, slots, BLOCK, 2, HEAD), bf16),
        ],
        in_specs=[far, far, far, anywhere],
        out_specs=[vmem, vmem, vmem],
        scratch_shapes=[
            pltpu.VMEM(state, f32), pltpu.VMEM(queries.shape, bf16),
            pltpu.SMEM((1,), i32), pltpu.SMEM((width,), i32), dma((3,)), dma((KV_CHUNKS, KVH)),
            dma((depth - 1,)), dma((depth - 1,)), dma((PLANE - 1,)), dma((PLANE - 1,)), dma((1,)), dma((1,)),
            dma((depth - 1,)), dma((depth - 1,)), dma((depth, PLANE - 1)), dma((depth, PLANE - 1)),
            dma((depth,)), dma((depth,)),
        ],
        compiler_params=params(collective_id=0),
    )(queries, lengths, block_table, kv_pool)
    parts = pl.pallas_call(
        functools.partial(attend_kernel, n, slots, width),
        out_shape=jax.ShapeDtypeStruct((n,) + state, bf16),
        in_specs=[vmem, anywhere, vmem],
        out_specs=vmem,
        scratch_shapes=[
            pltpu.VMEM((2 * BLOCK, HEAD), i32),
            pltpu.SMEM((n, 1, HEAD), i32),
            pltpu.SMEM((width,), i32), pltpu.SMEM((width,), i32), pltpu.SMEM((width,), i32),
            pltpu.SMEM((1,), i32), dma,
        ],
        compiler_params=params(),
    )(every_query.reshape((n,) + state), meta.reshape(n, 1, HEAD), kv)
    return pl.pallas_call(
        functools.partial(reduce_kernel, n),
        out_shape=jax.ShapeDtypeStruct(queries.shape, queries.dtype),
        in_specs=[vmem],
        out_specs=vmem,
        scratch_shapes=[
            pltpu.VMEM(state, f32),
            pltpu.VMEM((depth, PLANE) + state, bf16),
            pltpu.VMEM((depth, PLANE - 1) + state, bf16),
            pltpu.VMEM((depth, PLANE - 1) + state, bf16),
            pltpu.VMEM((depth,) + state, f32),
            pltpu.VMEM((depth - 1,) + state, bf16),
            pltpu.VMEM((depth - 1,) + state, bf16),
            pltpu.VMEM(state, f32),
            dma((depth,)), dma((depth,)), dma((depth, PLANE - 1)), dma((depth, PLANE - 1)),
            dma((depth - 1,)), dma((depth - 1,)),
        ],
        compiler_params=params(collective_id=1),
    )(parts.reshape(every.shape))


def solution(mesh):
    placed = (P("pool", None, None), P("pool", None, None, None), P("pool"), P("pool"))
    return jax.shard_map(
        functools.partial(body, mesh.shape["pool"]),
        mesh=mesh, in_specs=placed, out_specs=P("pool", None, None), check_vma=False,
    )
```
